256 devices in a mesh: dp: 32 (over z, y), mp: 8 (over x, core).
Axes of the slice: x: 4, y: 4, z: 8, core: 2. Of those that a mesh axis runs over, the one named last changes fastest.
Arguments:
- context: bfloat16 [64, 512, 3072], P('dp', None, 'mp'), may hold values from -0.625 to 0.625
- w_out: bfloat16 [3072, 6144], P('mp', 'dp'), may hold values from -0.109375 to 0.109375
- stream: bfloat16 [64, 512, 6144], P('dp', 'mp'), may hold values from -250 to 250
- gain: float32 [6144], replicated, may hold values from 0.1 to 1.9
- partner: int32 [64], replicated, may hold values from 0 to 63, as said below
Outputs:
- context_grad: bfloat16 [64, 512, 3072], P('dp', None, 'mp')
- weight_grad: float32 [3072, 6144], P('mp', 'dp')
- stream_grad: bfloat16 [64, 512, 6144], P('dp', 'mp')
The draws below stay inside these ranges and needn't reach their ends.
Inputs may be any that keep to these rules, and one draw needn't show every extreme that they name: partner pairs the views: partner[partner[i]] = i and partner[i] != i; which views pair is drawn afresh.
All inputs are finite; a program needn't handle non-finite values.
Results may differ from the reference program's by a relative error of at most 0.004.
The reference program's roundings to bfloat16 on the way (of `emb`) count: a program that leaves them out, or rounds other values in their place, can miss the bound.
Values may be sent and summed in bfloat16 or wider, within the bound.
A program may use at most 128 MiB of HBM per device.

```python
import jax
import jax.numpy as jnp
from jax import lax

D = 6144
SEQ = 512
HD = 3072
EMB = 64


def pairing(key):
    order = jax.random.permutation(key, EMB).astype(jnp.int32)
    first = order[0::2]
    second = order[1::2]
    count = jnp.arange(EMB // 2, dtype=jnp.int32)
    partner = jnp.zeros((EMB,), jnp.int32).at[first].set(second).at[second].set(first)
    couple = jnp.zeros((EMB,), jnp.int32).at[first].set(count).at[second].set(count)
    return (partner, couple)


def draw_partner(key, part):
    partner, couple = pairing(key)
    return partner


def draw_stream(key, part):
    partner, couple = pairing(key)
    key = jax.random.fold_in(key, 7)
    keys = jax.random.split(key, 5)
    shared = jnp.clip(jax.random.normal(keys[0], (EMB // 2, SEQ, D), jnp.float32), -6.0, 6.0)
    strength = jnp.exp(jax.random.uniform(keys[1], (EMB // 2,), jnp.float32, jnp.log(0.3), jnp.log(3.0)))
    noise = jnp.clip(jax.random.normal(keys[2], (EMB, SEQ, D), jnp.float32), -6.0, 6.0)
    columns = jnp.exp(jax.random.uniform(keys[3], (D,), jnp.float32, jnp.log(0.3), jnp.log(3.0)))
    rows = jnp.exp(jax.random.uniform(keys[4], (EMB, SEQ, 1), jnp.float32, jnp.log(0.3), jnp.log(3.0)))
    mixed = strength[couple][:, None, None] * shared[couple] + noise
    return (mixed * columns * rows).astype(jnp.bfloat16)


def shard_levels(key, shape, pieces, low, top_value):
    def one(position, blocks):
        heights = jax.random.uniform(jax.random.fold_in(jax.random.fold_in(key, 6), position), (blocks,), jnp.float32, low / len(pieces), top_value / len(pieces))
        return jnp.repeat(jnp.exp(heights), shape[position] // blocks).reshape((-1,) + (1,) * (len(shape) - position - 1))

    factor_of = one(*pieces[0])
    for cut in pieces[1:]:
        factor_of = factor_of * one(*cut)
    return factor_of


def centred(stream_key, extent, deviation, bound, pieces=(), kind=jnp.bfloat16):
    result = deviation * jax.random.normal(stream_key, extent, jnp.float32)
    if pieces:
        result = result * shard_levels(stream_key, extent, pieces, -0.22, 0.18)
    return jnp.clip(result, -bound, bound).astype(kind)


def setup_inputs(seed: int = 0) -> dict:
    key_list = jax.random.split(jax.random.key(seed), 6)
    context = centred(key_list[0], (EMB, SEQ, HD), 0.1, 0.625, ((0, 32), (2, 8)))
    w_out = centred(key_list[1], (HD, D), HD ** -0.5, 0.109375, ((0, 8), (1, 32)))
    stream = draw_stream(jax.random.fold_in(key_list[5], 71), 0)
    gain = jnp.clip(1.0 + 0.18 * jax.random.normal(key_list[3], (D,), jnp.float32), 0.1, 1.9)
    partner = draw_partner(jax.random.fold_in(key_list[5], 71), 0)
    return dict(context=context, w_out=w_out, stream=stream, gain=gain, partner=partner)


EPS = 1e-06
SHARP = 10.0
LOSS_MUL = 512.0

def pool_view(rows, gain):
    values = rows.astype(jnp.float32)
    rstd = lax.rsqrt(lax.optimization_barrier(jnp.mean(values * values, axis=-1, keepdims=True)) + EPS)
    return lax.optimization_barrier(jnp.sum(values * rstd * gain, axis=0)) / SEQ

def reference(context, w_out, stream, gain, partner):
    pooled = lax.map(lambda rows: pool_view(rows, gain), stream)
    inv = lax.rsqrt(lax.optimization_barrier(jnp.sum(pooled * pooled, axis=-1, keepdims=True)) + EPS)
    unit = pooled * inv
    emb = unit.astype(jnp.bfloat16)
    emb_values = emb.astype(jnp.float32)
    logits = SHARP * jnp.dot(emb, emb.T, preferred_element_type=jnp.float32)
    index = jnp.arange(EMB, dtype=jnp.int32)
    diagonal = index[:, None] == index[None, :]
    expo = jnp.where(diagonal, jnp.float32(0.0), jnp.exp(logits))
    total = lax.optimization_barrier(jnp.sum(expo, axis=1, keepdims=True))
    prob = expo / total
    target = (partner[:, None] == index[None, :]).astype(jnp.float32)
    dlog = LOSS_MUL * (prob - target)
    demb = SHARP * jnp.dot(dlog + dlog.T, emb_values, precision=lax.Precision.HIGHEST)
    dpooled = inv * (demb - unit * lax.optimization_barrier(jnp.sum(unit * demb, axis=-1, keepdims=True)))
    upstream = gain * dpooled / SEQ

    def one_view(carry, items):
        rows, above, ctx = items
        values = rows.astype(jnp.float32)
        rstd = lax.rsqrt(lax.optimization_barrier(jnp.mean(values * values, axis=-1, keepdims=True)) + EPS)
        inner = lax.optimization_barrier(jnp.mean(values * above[None, :], axis=-1, keepdims=True))
        grad_rows = (rstd * above[None, :] - values * (rstd * rstd * rstd) * inner).astype(jnp.bfloat16)
        ctx_grad = jnp.dot(grad_rows, w_out.T, preferred_element_type=jnp.float32).astype(jnp.bfloat16)
        carry = carry + jnp.dot(ctx.T, grad_rows, preferred_element_type=jnp.float32)
        return (carry, (ctx_grad, grad_rows))
    start = jnp.zeros((HD, D), jnp.float32)
    weight_grad, (context_grad, stream_grad) = lax.scan(one_view, start, (stream, upstream, context))
    return (context_grad, weight_grad, stream_grad)
```

```python
import jax
import jax.numpy as jnp
from jax import lax
from jax.experimental import pallas as pl
from jax.experimental.pallas import tpu as pltpu
from jax.sharding import PartitionSpec as P

EPS = 1e-06
SHARP = 10.0
LOSS_MUL = 512.0
D = 6144
SEQ = 512
HEADS = 384
VIEWS = 64
NZ, NY, NX = 8, 4, 4
MP = 8
OWN = 64
BLK = 768
PART = 192
HALF = PART // 2
PAY = PART + 16
PAYH = HALF + 16
F32 = jnp.float32
BF16 = jnp.bfloat16
I16 = jnp.int16
HIGH = lax.Precision.HIGHEST


def encode(values):
    top = jnp.max(jnp.abs(values), axis=0, keepdims=True)
    expo = jnp.ceil(16.0 * jnp.log2(jnp.maximum(top, 1e-30)))
    whole = jnp.round(values * jnp.exp2(14.9 - expo * 0.0625)).astype(jnp.int32).astype(I16)
    tail = jnp.broadcast_to(expo, (16, HEADS)).astype(jnp.int32).astype(I16)
    return whole, tail


def decode(ref, rows):
    expo = ref[pl.ds(rows, 16), :].astype(jnp.int32).astype(F32)[0:1, :]
    return ref[pl.ds(0, rows), :].astype(jnp.int32).astype(F32) * jnp.exp2(expo * 0.0625 - 14.9)


def put(ref, values, rows):
    whole, tail = encode(values)
    ref[pl.ds(0, rows), :] = whole
    ref[pl.ds(rows, 16), :] = tail


def kernel(
    ctx_hbm, w_hbm, stream_hbm, gain_ref, partner_ref,
    cg_hbm, wg_hbm, sg_hbm,
    G, SG, WT, CTX, CG, CGO, PB, WGO,
    EX1, UN, YB, ZB, E, LB, UPM, UPF, TM, TT, RB, CB,
    YS0, YR0, YS1, YR1, ZS0, ZR0, ZS1, ZR1,
    in_sem, out_sem, sgo_sem,
    xs_s, x_r, wy_s, wy_r, wz_s, wz_r,
    e1_s, e1_r, ey_s, ey_r, ez_s, ez_r, el_s, el_r, eu_s, eu_r, et_s, et_r,
    ys0_s, ys0_r, ys1_s, ys1_r, zs0_s, zs0_r, zs1_s, zs1_r,
):
    dp = lax.axis_index("dp")
    mp = lax.axis_index("mp")
    z, y = lax.div(dp, NY), lax.rem(dp, NY)
    x, core = lax.div(mp, 2), lax.rem(mp, 2)

    def zy(dz, dy):
        return lax.rem(z + (dz + NZ), NZ) * NY + lax.rem(y + (dy + NY), NY)

    def slot(dx, other):
        c = 1 - core if other else core
        return lax.rem(x + (dx + NX), NX) * 2 + c

    def near(dx=0, other=False, dz=0, dy=0):
        return (zy(dz, dy), slot(dx, other))

    def remote(src, dst, ss, rs, dev):
        return pltpu.make_async_remote_copy(
            src_ref=src, dst_ref=dst, send_sem=ss, recv_sem=rs,
            device_id=dev, device_id_type=pl.DeviceIdType.MESH,
        )

    own_rows = pl.ds(pl.multiple_of(mp * OWN, OWN), OWN)
    load_stream = pltpu.make_async_copy(stream_hbm, G.at[:, own_rows, :], in_sem.at[0])
    load_ctx = pltpu.make_async_copy(ctx_hbm, CTX, in_sem.at[1])
    load_w = pltpu.make_async_copy(
        w_hbm, WT.at[pl.ds(pl.multiple_of(dp * PART, PART), PART), :], in_sem.at[2]
    )
    load_stream.start()
    load_w.start()
    load_ctx.start()

    barrier = pltpu.get_barrier_semaphore()
    peers = [(dp, lax.rem(mp + d, MP)) for d in range(1, MP)]
    ypeers = [near(dy=d) for d in range(1, NY)]
    zpeers = [near(dz=d) for d in range(1, NZ)]
    for dev in peers + ypeers + zpeers:
        pl.semaphore_signal(barrier, inc=1, device_id=dev, device_id_type=pl.DeviceIdType.MESH)

    def zblock(k):
        dist = lax.div(NZ - k, 2)
        odd = lax.rem(k, 2)
        return lax.rem(z + NZ + (2 * odd - 1) * dist, NZ)

    def cols(k):
        return pl.ds(pl.multiple_of(zblock(k) * BLK, BLK), BLK)

    def rows(s):
        return pl.ds(pl.multiple_of(s * OWN, OWN), OWN)

    def x_own(k, t):
        ref = G.at[:, own_rows, cols(k)]
        dev = (near(dx=1), near(dx=-1), near(other=True))[t]
        return remote(ref, ref, xs_s.at[k, t], x_r.at[k, t], dev)

    def x_fwd(k, t):
        if t == 0:
            ref = G.at[0, rows(slot(-1, False)), cols(k)]
            return remote(ref, ref, xs_s.at[k, 3], x_r.at[k, 3], near(dx=1))
        ref = G.at[1, rows(slot(1, False)), cols(k)]
        return remote(ref, ref, xs_s.at[k, 4], x_r.at[k, 4], near(dx=-1))

    def x_sib(k, t):
        ref = G.at[:, rows(slot((-1, 1, 2)[t], False)), cols(k)]
        return remote(ref, ref, xs_s.at[k, 5 + t], x_r.at[k, 5 + t], near(other=True))

    def x_wait(k, t):
        if t < 3:
            ref = G.at[:, rows((slot(-1, False), slot(1, False), slot(0, True))[t]), cols(k)]
        elif t < 5:
            ref = G.at[t - 3, rows(slot(2, False)), cols(k)]
        else:
            ref = G.at[:, rows(slot((-1, 1, 2)[t - 5], True)), cols(k)]
        remote(ref, ref, xs_s.at[k, t], x_r.at[k, t], near(other=True)).wait_recv()

    def x_send(k):
        for t in range(3):
            x_own(k, t).start()

    def x_forward(k):
        x_wait(k, 0)
        x_fwd(k, 0).start()
        x_sib(k, 0).start()
        x_wait(k, 1)
        x_fwd(k, 1).start()
        x_sib(k, 1).start()

    def x_opposite(k):
        x_wait(k, 3)
        x_wait(k, 4)
        x_sib(k, 2).start()

    def x_arrived(k):
        x_wait(k, 2)
        for t in (5, 6, 7):
            x_wait(k, t)

    def wy_copy(d):
        ref = WT.at[pl.ds(pl.multiple_of(dp * PART, PART), PART), :]
        return remote(ref, ref, wy_s.at[d - 1], wy_r.at[y], near(dy=d))

    def wy_wait(d):
        s = lax.rem(y + d, NY)
        ref = WT.at[pl.ds(pl.multiple_of((z * NY + s) * PART, PART), PART), :]
        remote(ref, ref, wy_s.at[d - 1], wy_r.at[s], near(dy=d)).wait_recv()

    def wz_ref(bundle, f, t):
        start = pl.multiple_of(bundle * BLK, BLK)
        if f == 3:
            return WT.at[pl.ds(pl.multiple_of(start + t * (BLK // 2), BLK // 2), BLK // 2), :]
        return WT.at[pl.ds(start, BLK), :]

    def wz_copy(f, t):
        step = f if t else NZ - f
        ref = wz_ref(lax.rem(z + step, NZ), f, t)
        return remote(ref, ref, wz_s.at[f, t], wz_r.at[f, t], near(dz=-1 if t else 1))

    def wz_wait(f, t):
        step = f + 1 if t else NZ - f - 1
        ref = wz_ref(lax.rem(z + step, NZ), f, t)
        remote(ref, ref, wz_s.at[f, t], wz_r.at[f, t], near(dz=1)).wait_recv()

    def wz_next(f):
        for t in range(2):
            wz_wait(f - 1, t)
            wz_copy(f, t).start()

    def ex(buf, ss, rs, d):
        ref = buf.at[mp]
        return remote(ref, ref, ss.at[d - 1], rs.at[mp], (dp, lax.rem(mp + d, MP)))

    def ex_send(buf, ss, rs):
        for d in (4, 2, 3, 5, 6, 7, 1):
            ex(buf, ss, rs, d).start()

    def ex_wait(buf, ss, rs):
        for d in range(1, MP):
            s = lax.rem(mp + d, MP)
            ref = buf.at[s]
            remote(ref, ref, ss.at[d - 1], rs.at[s], (dp, s)).wait_recv()

    def ey_copy(d):
        ref = YB.at[y]
        return remote(ref, ref, ey_s.at[d - 1], ey_r.at[y], near(dy=d))

    def ez_copy(d):
        ref = ZB.at[z]
        return remote(ref, ref, ez_s.at[d - 1], ez_r.at[z], near(dz=d))

    load_stream.wait()

    def rstd_of(v):
        acc = jnp.zeros((OWN, 128), F32)
        for q in range(D // 128):
            part = G[v, own_rows, pl.ds(q * 128, 128)].astype(F32)
            acc = acc + part * part
        mean = jnp.sum(acc, axis=1, keepdims=True) * (1.0 / D)
        return lax.rsqrt(mean + EPS)

    rstd = [rstd_of(v) for v in range(2)]
    for v in range(2):
        for q in range(MP):
            part = G[v, own_rows, pl.ds(q * BLK, BLK)].astype(F32)
            EX1[mp, v, pl.ds(q, 1), :] = jnp.sum(part * rstd[v], axis=0, keepdims=True)

    pl.semaphore_wait(barrier, (MP - 1) + (NY - 1) + (NZ - 1))
    ex_send(EX1, e1_s, e1_r)
    load_w.wait()
    for d in (2, 1, 3):
        wy_copy(d).start()
    x_send(0)
    x_send(1)
    ex_wait(EX1, e1_s, e1_r)

    gain8 = gain_ref[...]
    squares = []
    for v in range(2):
        total = EX1[0, v]
        for s in range(1, MP):
            total = total + EX1[s, v]
        pooled = total * gain8 * (1.0 / SEQ)
        UN[v] = pooled
        sq = jnp.sum(jnp.sum(pooled * pooled, axis=1, keepdims=True), axis=0, keepdims=True)
        squares.append(lax.rsqrt(sq + EPS))
    unit = [UN[v, pl.ds(mp, 1), :] * squares[v] for v in range(2)]
    emb = [u.astype(BF16).astype(F32) for u in unit]
    row8 = lax.broadcasted_iota(jnp.int32, (8, BLK), 0)
    zero8 = jnp.zeros((8, BLK), F32)

    def two(a, b, first):
        return jnp.where(row8 == first, a, jnp.where(row8 == first + 1, b, zero8))

    YB[y] = two(emb[0], emb[1], 2 * y)
    for d in (2, 1, 3):
        ey_copy(d).start()
    unit8 = two(unit[0], unit[1], 0)
    for d in range(1, NY):
        s = lax.rem(y + d, NY)
        ref = YB.at[s]
        remote(ref, ref, ey_s.at[d - 1], ey_r.at[s], near(dy=d)).wait_recv()
    eight = YB[0] + YB[1] + YB[2] + YB[3]
    ZB[z] = jnp.concatenate([eight[:, 0:HEADS], eight[:, HEADS:BLK]], axis=0).astype(BF16)
    for d in (4, 3, 5, 2, 6, 1, 7):
        ez_copy(d).start()
    for d in range(1, NY):
        wy_wait(d)
    for t in range(2):
        wz_copy(0, t).start()
    x_send(2)
    for d in range(1, NZ):
        s = lax.rem(z + d, NZ)
        ref = ZB.at[s]
        remote(ref, ref, ez_s.at[d - 1], ez_r.at[s], near(dz=d)).wait_recv()
    for s in range(NZ):
        part = ZB[s].astype(F32)
        E[pl.ds(8 * s, 8), pl.ds(0, HEADS)] = part[0:8]
        E[pl.ds(8 * s, 8), pl.ds(HEADS, HEADS)] = part[8:16]

    every = E[...]
    small = every.astype(BF16)
    contract = (((1,), (1,)), ((), ()))
    raw = lax.dot_general(small, small, contract, preferred_element_type=F32)
    cross = lax.dot_general(unit8, every, contract, precision=HIGH, preferred_element_type=F32)
    LB[mp, pl.ds(0, 32), pl.ds(0, 64)] = raw[0:32]
    LB[mp, pl.ds(0, 32), pl.ds(64, 64)] = raw[32:64]
    LB[mp, pl.ds(32, 8), pl.ds(0, 64)] = cross
    LB[mp, pl.ds(32, 8), pl.ds(64, 64)] = jnp.zeros((8, 64), F32)
    ex_send(LB, el_s, el_r)
    x_forward(0)
    x_send(3)
    ex_wait(LB, el_s, el_r)
    summed = LB[0]
    for s in range(1, MP):
        summed = summed + LB[s]
    logits = SHARP * jnp.concatenate([summed[0:32, 0:64], summed[0:32, 64:128]], axis=0)
    cross = summed[32:40, 0:64]

    rowi = lax.broadcasted_iota(jnp.int32, (VIEWS, VIEWS), 0)
    coli = lax.broadcasted_iota(jnp.int32, (VIEWS, VIEWS), 1)
    expo = jnp.where(rowi == coli, jnp.float32(0.0), jnp.exp(logits))
    both = expo / jnp.sum(expo, axis=1, keepdims=True) + expo / jnp.sum(expo, axis=0, keepdims=True)
    lane = lax.broadcasted_iota(jnp.int32, (1, VIEWS), 1)
    coef = []
    for v in range(2):
        index = 2 * dp + v
        mine = jnp.sum(jnp.where(rowi == index, both, 0.0), axis=0, keepdims=True)
        target = jnp.where(lane == partner_ref[index], jnp.float32(2.0), jnp.float32(0.0))
        coef.append(LOSS_MUL * (mine - target))
    r64 = lax.broadcasted_iota(jnp.int32, (8, VIEWS), 0)
    coef8 = jnp.where(r64 == 0, coef[0], jnp.where(r64 == 1, coef[1], jnp.zeros((8, VIEWS), F32)))
    demb = SHARP * jnp.dot(coef8, every, precision=HIGH, preferred_element_type=F32)
    along = SHARP * jnp.sum(coef8 * cross, axis=1, keepdims=True)
    inv8 = two(jnp.broadcast_to(squares[0], (1, BLK)), jnp.broadcast_to(squares[1], (1, BLK)), 0)
    dpooled = inv8 * (demb - unit8 * along)
    up8 = gain_ref[pl.ds(mp, 1), :] * dpooled * (1.0 / SEQ)
    UPM[mp] = jnp.zeros((8, 256), F32)
    for v in range(2):
        for c in range(3):
            UPM[mp, pl.ds(3 * v + c, 1), :] = up8[v : v + 1, 256 * c : 256 * (c + 1)]
    ex_send(UPM, eu_s, eu_r)
    x_opposite(0)
    x_forward(1)
    x_send(4)
    ex_wait(UPM, eu_s, eu_r)
    for s in range(MP):
        for v in range(2):
            for c in range(3):
                UPF[v, :, pl.ds(s * BLK + 256 * c, 256)] = UPM[s, pl.ds(3 * v + c, 1), :]

    diag = lax.broadcasted_iota(jnp.int32, (OWN, OWN), 0) == lax.broadcasted_iota(jnp.int32, (OWN, OWN), 1)
    TM[mp] = jnp.zeros((8, 128), F32)
    for v in range(2):
        acc = jnp.zeros((OWN, 128), F32)
        for q in range(D // 128):
            part = G[v, own_rows, pl.ds(q * 128, 128)].astype(F32)
            acc = acc + part * UPF[v, :, pl.ds(q * 128, 128)]
        inner = jnp.sum(acc, axis=1, keepdims=True) * (1.0 / D)
        slope = rstd[v] * rstd[v] * rstd[v] * inner
        for r, column in enumerate((rstd[v], slope)):
            line = jnp.sum(jnp.where(diag, column, 0.0), axis=0, keepdims=True)
            TM[mp, pl.ds(r, 1), pl.ds(v * OWN, OWN)] = line
    ex_send(TM, et_s, et_r)
    load_ctx.wait()
    CG[...] = jnp.zeros_like(CG)
    ex_wait(TM, et_s, et_r)
    for s in range(MP):
        TT[pl.ds(8 * s, 8), :] = TM[s]
    TT[pl.ds(64, 64), :] = jnp.zeros((64, 128), F32)
    flat = TT[...].T
    for s in range(MP):
        for v in range(2):
            piece = flat[v * OWN : (v + 1) * OWN]
            RB[v, pl.ds(s * OWN, OWN), :] = jnp.broadcast_to(piece[:, 8 * s : 8 * s + 1], (OWN, 128))
            CB[v, pl.ds(s * OWN, OWN), :] = jnp.broadcast_to(piece[:, 8 * s + 1 : 8 * s + 2], (OWN, 128))

    def part_rows(dy):
        return pl.ds(pl.multiple_of(lax.rem(y + dy, NY) * PART, PART), PART)

    def half_rows(dy, h):
        start = lax.rem(y + dy, NY) * PART + h * HALF
        return pl.ds(pl.multiple_of(start, HALF), HALF)

    def ys0(k, h):
        return remote(YS0.at[k, h], YR0.at[k, h], ys0_s.at[k, h], ys0_r.at[k, h], near(dy=1 if h == 0 else -1))

    def ys1(k, h):
        return remote(YS1.at[k, h], YR1.at[k, h], ys1_s.at[k, h], ys1_r.at[k, h], near(dy=1 if h == 0 else -1))

    def zs0(h):
        return remote(ZS0.at[h], ZR0.at[h], zs0_s.at[h], zs0_r.at[h], near(dz=1 if h == 0 else -1))

    def zs1(k):
        odd = lax.rem(k, 2)
        target = lax.rem(z + NZ - 1 + 2 * odd, NZ) * NY + y
        return remote(ZS1.at[k], ZR1.at[k], zs1_s.at[k], zs1_r.at[k], (target, mp))

    def sgout(k):
        return pltpu.make_async_copy(SG.at[:, own_rows, cols(k)], sg_hbm.at[:, :, cols(k)], sgo_sem.at[k])

    def block(k):
        first = zblock(k) * BLK
        x_arrived(k)

        def build(g, carry):
            v = lax.div(g, MP)
            r = rows(lax.rem(g, MP))
            rs = RB[v, r, :]
            cs = CB[v, r, :]
            for l in range(BLK // 128):
                c = pl.ds(pl.multiple_of(first + l * 128, 128), 128)
                value = G[v, r, c].astype(F32)
                SG[v, r, c] = (rs * UPF[v, :, c] - value * cs).astype(BF16)
            return carry

        lax.fori_loop(0, 2 * MP, build, 0)
        sgout(k).start()
        keep = lax.rem(k, 3)

        def matmul(m, carry):
            c = pl.ds(pl.multiple_of(first + m * 256, 256), 256)
            left = SG[:, :, c].reshape(2 * SEQ, 256)
            right = CTX[...].reshape(2 * SEQ, HEADS)
            PB[keep, pl.ds(pl.multiple_of(m * 256, 256), 256), :] = lax.dot_general(
                left, right, (((0,), (0,)), ((), ())), preferred_element_type=F32
            )
            return carry

        lax.fori_loop(0, 3, matmul, 0)
        for h in range(2):
            put(YS0.at[k, h], PB[keep, half_rows(2, h), :], HALF)
            ys0(k, h).start()

    def y_second(k):
        keep = lax.rem(k, 3)
        for h in range(2):
            ys0(k, h).wait_recv()
            spot = half_rows(1 if h == 0 else 3, h)
            PB[keep, spot, :] = PB[keep, spot, :] + decode(YR0.at[k, h], HALF)
            put(YS1.at[k, h], PB[keep, part_rows(1 if h == 0 else 3), :], PART)
            ys1(k, h).start()

    def z_part(k):
        keep = lax.rem(k, 3)
        ys1(k, 0).wait_recv()
        ys1(k, 1).wait_recv()
        spot = part_rows(0)
        PB[keep, spot, :] = PB[keep, spot, :] + decode(YR1.at[k, 0], PART) + decode(YR1.at[k, 1], PART)

        @pl.when(k == 0)
        def _():
            for h in range(2):
                put(ZS0.at[h], PB[keep, half_rows(0, h), :], HALF)
                zs0(h).start()

        for h in range(2):
            @pl.when(k == 1 + h)
            def _():
                zs0(h).wait_recv()
                half = half_rows(0, h)
                PB[keep, half, :] = PB[keep, half, :] + decode(ZR0.at[h], HALF)

        @pl.when(jnp.logical_and(k >= 3, k <= 6))
        def _():
            zs1(k - 2).wait_recv()
            PB[keep, spot, :] = PB[keep, spot, :] + decode(ZR1.at[k - 2], PART)

        @pl.when(jnp.logical_and(k >= 1, k <= 6))
        def _():
            put(ZS1.at[k], PB[keep, spot, :], PART)
            zs1(k).start()

        @pl.when(k == 7)
        def _():
            zs1(5).wait_recv()
            zs1(6).wait_recv()
            WGO[...] = PB[keep, spot, :] + decode(ZR1.at[5], PART) + decode(ZR1.at[6], PART)

    def project(b):
        first = zblock(b) * BLK

        def step(m, carry):
            v = lax.div(m, 2)
            r = pl.ds(pl.multiple_of(lax.rem(m, 2) * 256, 256), 256)
            left = SG[v, r, pl.ds(pl.multiple_of(first, BLK), BLK)]
            right = WT[pl.ds(pl.multiple_of(first, BLK), BLK), :]
            CG[v, r, :] = CG[v, r, :] + jnp.dot(left, right, preferred_element_type=F32)
            return carry

        lax.fori_loop(0, 4, step, 0)

    def iteration(k, carry):
        @pl.when(k <= 2)
        def _():
            x_send(k + 5)

        @pl.when(k <= 5)
        def _():
            x_forward(k + 2)

        @pl.when(k <= 6)
        def _():
            x_opposite(k + 1)

        for f in range(1, 4):
            @pl.when(k == 2 * f - 2)
            def _():
                wz_next(f)

        @pl.when(k <= 7)
        def _():
            block(k)

        @pl.when(jnp.logical_and(k >= 1, k <= 8))
        def _():
            y_second(k - 1)

        @pl.when(k >= 2)
        def _():
            z_part(k - 2)

        @pl.when(jnp.logical_and(k >= 4, k <= 5))
        def _():
            project(k - 1)

        @pl.when(jnp.logical_and(k >= 6, k <= 7))
        def _():
            project(k - 5)

        @pl.when(k == 8)
        def _():
            project(5)
            project(6)
            project(7)
            wz_wait(3, 0)
            wz_wait(3, 1)
            project(0)
            CGO[...] = CG[...].astype(BF16)
            pltpu.make_async_copy(CGO, cg_hbm, out_sem.at[0]).start()

        return carry

    lax.fori_loop(0, 10, iteration, 0)
    wg_out = pltpu.make_async_copy(WGO, wg_hbm, out_sem.at[1])
    wg_out.start()

    def drain(k, carry):
        for t in range(3):
            x_own(k, t).wait_send()
            x_sib(k, t).wait_send()
        for h in range(2):
            x_fwd(k, h).wait_send()
            ys0(k, h).wait_send()
            ys1(k, h).wait_send()
        sgout(k).wait()

        @pl.when(jnp.logical_and(k >= 1, k <= 6))
        def _():
            zs1(k).wait_send()

        return carry

    lax.fori_loop(0, NZ, drain, 0)
    for h in range(2):
        zs0(h).wait_send()
    for d in range(1, NY):
        wy_copy(d).wait_send()
        ey_copy(d).wait_send()
    for f in range(4):
        for t in range(2):
            wz_copy(f, t).wait_send()
    for d in range(1, NZ):
        ez_copy(d).wait_send()
    for d in range(1, MP):
        ex(EX1, e1_s, e1_r, d).wait_send()
        ex(LB, el_s, el_r, d).wait_send()
        ex(UPM, eu_s, eu_r, d).wait_send()
        ex(TM, et_s, et_r, d).wait_send()
    pltpu.make_async_copy(CGO, cg_hbm, out_sem.at[0]).wait()
    wg_out.wait()


def local(context, w_out, stream, gain, partner):
    anywhere = pl.BlockSpec(memory_space=pl.ANY)
    sems = pltpu.SemaphoreType.DMA
    vm = pltpu.VMEM
    scratch = [
        vm((2, SEQ, D), BF16), vm((2, SEQ, D), BF16), vm((D, HEADS), BF16), vm((2, SEQ, HEADS), BF16),
        vm((2, SEQ, HEADS), F32), vm((2, SEQ, HEADS), BF16), vm((3, BLK, HEADS), F32), vm((PART, HEADS), F32),
        vm((MP, 2, MP, BLK), F32), vm((2, MP, BLK), F32), vm((NY, 8, BLK), F32), vm((NZ, 16, HEADS), BF16),
        vm((VIEWS, BLK), F32), vm((MP, 40, 128), F32), vm((MP, 8, 256), F32), vm((2, 1, D), F32),
        vm((MP, 8, 128), F32), vm((128, 128), F32), vm((2, SEQ, 128), F32), vm((2, SEQ, 128), F32),
        vm((NZ, 2, PAYH, HEADS), I16), vm((NZ, 2, PAYH, HEADS), I16),
        vm((NZ, 2, PAY, HEADS), I16), vm((NZ, 2, PAY, HEADS), I16),
        vm((2, PAYH, HEADS), I16), vm((2, PAYH, HEADS), I16),
        vm((NZ, PAY, HEADS), I16), vm((NZ, PAY, HEADS), I16),
        sems((3,)), sems((2,)), sems((NZ,)),
        sems((NZ, 8)), sems((NZ, 8)), sems((NY - 1,)), sems((NY,)), sems((4, 2)), sems((4, 2)),
        sems((MP - 1,)), sems((MP,)), sems((NY - 1,)), sems((NY,)), sems((NZ - 1,)), sems((NZ,)),
        sems((MP - 1,)), sems((MP,)), sems((MP - 1,)), sems((MP,)), sems((MP - 1,)), sems((MP,)),
        sems((NZ, 2)), sems((NZ, 2)), sems((NZ, 2)), sems((NZ, 2)),
        sems((2,)), sems((2,)), sems((NZ,)), sems((NZ,)),
    ]
    context_grad, weight_grad, stream_grad = pl.pallas_call(
        kernel,
        out_shape=(
            jax.ShapeDtypeStruct(context.shape, BF16),
            jax.ShapeDtypeStruct((PART, HEADS), F32),
            jax.ShapeDtypeStruct(stream.shape, BF16),
        ),
        in_specs=[
            anywhere, anywhere, anywhere,
            pl.BlockSpec(memory_space=pltpu.VMEM),
            pl.BlockSpec(memory_space=pltpu.SMEM),
        ],
        out_specs=[anywhere] * 3,
        scratch_shapes=scratch,
        compiler_params=pltpu.CompilerParams(
            collective_id=0, has_side_effects=True, vmem_limit_bytes=60 * 2**20
        ),
        cost_estimate=pl.CostEstimate(flops=10**10, bytes_accessed=6 * 10**6, transcendentals=0),
    )(context, w_out.T, stream, gain.reshape(MP, BLK), partner)
    return context_grad, weight_grad.T, stream_grad


def solution(mesh):
    placed = (P("dp", None, "mp"), P("mp", "dp"), P("dp", "mp", None), P(), P())
    return jax.shard_map(
        local,
        mesh=mesh,
        in_specs=placed,
        out_specs=(P("dp", None, "mp"), P("mp", "dp"), P("dp", "mp", None)),
        check_vma=False,
    )
```

```python
import jax
import jax.numpy as jnp
from jax import lax
from jax.experimental import pallas as pl
from jax.experimental.pallas import tpu as pltpu
from jax.sharding import PartitionSpec as P

EPS = 1e-06
SHARP = 10.0
LOSS_MUL = 512.0
D = 6144
SEQ = 512
HEADS = 384
VIEWS = 64
NZ, NY, NX = 8, 4, 4
MP = 8
OWN = 64
BLK = 768
PART = 192
HALF = PART // 2
PAY = PART + 16
PAYH = HALF + 16
F32 = jnp.float32
BF16 = jnp.bfloat16
I16 = jnp.int16
HIGH = lax.Precision.HIGHEST


def encode(values):
    top = jnp.max(jnp.abs(values), axis=0, keepdims=True)
    expo = jnp.ceil(16.0 * jnp.log2(jnp.maximum(top, 1e-30)))
    whole = jnp.round(values * jnp.exp2(14.9 - expo * 0.0625)).astype(jnp.int32).astype(I16)
    tail = jnp.broadcast_to(expo, (16, HEADS)).astype(jnp.int32).astype(I16)
    return whole, tail


def decode(ref, rows):
    expo = ref[pl.ds(rows, 16), :].astype(jnp.int32).astype(F32)[0:1, :]
    return ref[pl.ds(0, rows), :].astype(jnp.int32).astype(F32) * jnp.exp2(expo * 0.0625 - 14.9)


def put(ref, values, rows):
    whole, tail = encode(values)
    ref[pl.ds(0, rows), :] = whole
    ref[pl.ds(rows, 16), :] = tail


def kernel(
    ctx_hbm, w_hbm, stream_hbm, gain_ref, partner_ref,
    cg_hbm, wg_hbm, sg_hbm,
    G, SG, WT, CTX, CG, CGO, PB, WGO,
    EX1, UN, YB, ZB, E, LB, UPM, UPF, TM, TT, RB, CB,
    YS0, YR0, YS1, YR1, ZS0, ZR0, ZS1, ZR1,
    in_sem, out_sem, sgo_sem,
    xs_s, x_r, wy_s, wy_r, wz_s, wz_r,
    e1_s, e1_r, ey_s, ey_r, ez_s, ez_r, el_s, el_r, eu_s, eu_r, et_s, et_r,
    ys0_s, ys0_r, ys1_s, ys1_r, zs0_s, zs0_r, zs1_s, zs1_r,
):
    dp = lax.axis_index("dp")
    mp = lax.axis_index("mp")
    z, y = lax.div(dp, NY), lax.rem(dp, NY)
    x, core = lax.div(mp, 2), lax.rem(mp, 2)

    def zy(dz, dy):
        return lax.rem(z + (dz + NZ), NZ) * NY + lax.rem(y + (dy + NY), NY)

    def slot(dx, other):
        c = 1 - core if other else core
        return lax.rem(x + (dx + NX), NX) * 2 + c

    def near(dx=0, other=False, dz=0, dy=0):
        return (zy(dz, dy), slot(dx, other))

    def remote(src, dst, ss, rs, dev):
        return pltpu.make_async_remote_copy(
            src_ref=src, dst_ref=dst, send_sem=ss, recv_sem=rs,
            device_id=dev, device_id_type=pl.DeviceIdType.MESH,
        )

    own_rows = pl.ds(pl.multiple_of(mp * OWN, OWN), OWN)
    load_stream = pltpu.make_async_copy(stream_hbm, G.at[:, own_rows, :], in_sem.at[0])
    load_ctx = pltpu.make_async_copy(ctx_hbm, CTX, in_sem.at[1])
    load_w = pltpu.make_async_copy(
        w_hbm, WT.at[pl.ds(pl.multiple_of(dp * PART, PART), PART), :], in_sem.at[2]
    )
    load_stream.start()
    load_w.start()
    load_ctx.start()

    barrier = pltpu.get_barrier_semaphore()
    peers = [(dp, lax.rem(mp + d, MP)) for d in range(1, MP)]
    ypeers = [near(dy=d) for d in range(1, NY)]
    zpeers = [near(dz=d) for d in range(1, NZ)]
    for dev in peers + ypeers + zpeers:
        pl.semaphore_signal(barrier, inc=1, device_id=dev, device_id_type=pl.DeviceIdType.MESH)

    def zblock(k):
        dist = lax.div(NZ - k, 2)
        odd = lax.rem(k, 2)
        return lax.rem(z + NZ + (2 * odd - 1) * dist, NZ)

    def cols(k):
        return pl.ds(pl.multiple_of(zblock(k) * BLK, BLK), BLK)

    def rows(s):
        return pl.ds(pl.multiple_of(s * OWN, OWN), OWN)

    def x_own(k, t):
        ref = G.at[:, own_rows, cols(k)]
        dev = (near(dx=1), near(dx=-1), near(other=True))[t]
        return remote(ref, ref, xs_s.at[k, t], x_r.at[k, t], dev)

    def x_fwd(k, t):
        if t == 0:
            ref = G.at[0, rows(slot(-1, False)), cols(k)]
            return remote(ref, ref, xs_s.at[k, 3], x_r.at[k, 3], near(dx=1))
        ref = G.at[1, rows(slot(1, False)), cols(k)]
        return remote(ref, ref, xs_s.at[k, 4], x_r.at[k, 4], near(dx=-1))

    def x_sib(k, t):
        ref = G.at[:, rows(slot((-1, 1, 2)[t], False)), cols(k)]
        return remote(ref, ref, xs_s.at[k, 5 + t], x_r.at[k, 5 + t], near(other=True))

    def x_wait(k, t):
        if t < 3:
            ref = G.at[:, rows((slot(-1, False), slot(1, False), slot(0, True))[t]), cols(k)]
        elif t < 5:
            ref = G.at[t - 3, rows(slot(2, False)), cols(k)]
        else:
            ref = G.at[:, rows(slot((-1, 1, 2)[t - 5], True)), cols(k)]
        remote(ref, ref, xs_s.at[k, t], x_r.at[k, t], near(other=True)).wait_recv()

    def x_send(k):
        for t in range(3):
            x_own(k, t).start()

    def x_forward(k):
        x_wait(k, 0)
        x_fwd(k, 0).start()
        x_sib(k, 0).start()
        x_wait(k, 1)
        x_fwd(k, 1).start()
        x_sib(k, 1).start()

    def x_opposite(k):
        x_wait(k, 3)
        x_wait(k, 4)
        x_sib(k, 2).start()

    def x_arrived(k):
        x_wait(k, 2)
        for t in (5, 6, 7):
            x_wait(k, t)

    def wy_copy(d):
        ref = WT.at[pl.ds(pl.multiple_of(dp * PART, PART), PART), :]
        return remote(ref, ref, wy_s.at[d - 1], wy_r.at[y], near(dy=d))

    def wy_wait(d):
        s = lax.rem(y + d, NY)
        ref = WT.at[pl.ds(pl.multiple_of((z * NY + s) * PART, PART), PART), :]
        remote(ref, ref, wy_s.at[d - 1], wy_r.at[s], near(dy=d)).wait_recv()

    def wz_ref(bundle, f, t):
        start = pl.multiple_of(bundle * BLK, BLK)
        if f == 3:
            return WT.at[pl.ds(pl.multiple_of(start + t * (BLK // 2), BLK // 2), BLK // 2), :]
        return WT.at[pl.ds(start, BLK), :]

    def wz_copy(f, t):
        step = f if t else NZ - f
        ref = wz_ref(lax.rem(z + step, NZ), f, t)
        return remote(ref, ref, wz_s.at[f, t], wz_r.at[f, t], near(dz=-1 if t else 1))

    def wz_wait(f, t):
        step = f + 1 if t else NZ - f - 1
        ref = wz_ref(lax.rem(z + step, NZ), f, t)
        remote(ref, ref, wz_s.at[f, t], wz_r.at[f, t], near(dz=1)).wait_recv()

    def wz_next(f):
        for t in range(2):
            wz_wait(f - 1, t)
            wz_copy(f, t).start()

    def ex(buf, ss, rs, d):
        ref = buf.at[mp]
        return remote(ref, ref, ss.at[d - 1], rs.at[mp], (dp, lax.rem(mp + d, MP)))

    def ex_send(buf, ss, rs):
        for d in (4, 2, 3, 5, 6, 7, 1):
            ex(buf, ss, rs, d).start()

    def ex_wait(buf, ss, rs):
        for d in range(1, MP):
            s = lax.rem(mp + d, MP)
            ref = buf.at[s]
            remote(ref, ref, ss.at[d - 1], rs.at[s], (dp, s)).wait_recv()

    def ey_copy(d):
        ref = YB.at[y]
        return remote(ref, ref, ey_s.at[d - 1], ey_r.at[y], near(dy=d))

    def ez_copy(d):
        ref = ZB.at[z]
        return remote(ref, ref, ez_s.at[d - 1], ez_r.at[z], near(dz=d))

    load_stream.wait()

    def rstd_of(v):
        acc = jnp.zeros((OWN, 128), F32)
        for q in range(D // 128):
            part = G[v, own_rows, pl.ds(q * 128, 128)].astype(F32)
            acc = acc + part * part
        mean = jnp.sum(acc, axis=1, keepdims=True) * (1.0 / D)
        return lax.rsqrt(mean + EPS)

    rstd = [rstd_of(v) for v in range(2)]
    for v in range(2):
        for q in range(MP):
            part = G[v, own_rows, pl.ds(q * BLK, BLK)].astype(F32)
            EX1[mp, v, pl.ds(q, 1), :] = jnp.sum(part * rstd[v], axis=0, keepdims=True)

    pl.semaphore_wait(barrier, (MP - 1) + (NY - 1) + (NZ - 1))
    ex_send(EX1, e1_s, e1_r)
    load_w.wait()
    for d in (2, 1, 3):
        wy_copy(d).start()
    x_send(0)
    x_send(1)
    ex_wait(EX1, e1_s, e1_r)

    gain8 = gain_ref[...]
    squares = []
    for v in range(2):
        total = EX1[0, v]
        for s in range(1, MP):
            total = total + EX1[s, v]
        pooled = total * gain8 * (1.0 / SEQ)
        UN[v] = pooled
        sq = jnp.sum(jnp.sum(pooled * pooled, axis=1, keepdims=True), axis=0, keepdims=True)
        squares.append(lax.rsqrt(sq + EPS))
    unit = [UN[v, pl.ds(mp, 1), :] * squares[v] for v in range(2)]
    emb = [u.astype(BF16).astype(F32) for u in unit]
    row8 = lax.broadcasted_iota(jnp.int32, (8, BLK), 0)
    zero8 = jnp.zeros((8, BLK), F32)

    def two(a, b, first):
        return jnp.where(row8 == first, a, jnp.where(row8 == first + 1, b, zero8))

    YB[y] = two(emb[0], emb[1], 2 * y)
    for d in (2, 1, 3):
        ey_copy(d).start()
    unit8 = two(unit[0], unit[1], 0)
    for d in range(1, NY):
        s = lax.rem(y + d, NY)
        ref = YB.at[s]
        remote(ref, ref, ey_s.at[d - 1], ey_r.at[s], near(dy=d)).wait_recv()
    eight = YB[0] + YB[1] + YB[2] + YB[3]
    ZB[z] = jnp.concatenate([eight[:, 0:HEADS], eight[:, HEADS:BLK]], axis=0).astype(BF16)
    for d in (4, 3, 5, 2, 6, 1, 7):
        ez_copy(d).start()
    for d in range(1, NY):
        wy_wait(d)
    for t in range(2):
        wz_copy(0, t).start()
    x_forward(0)
    x_send(2)
    for d in range(1, NZ):
        s = lax.rem(z + d, NZ)
        ref = ZB.at[s]
        remote(ref, ref, ez_s.at[d - 1], ez_r.at[s], near(dz=d)).wait_recv()
    for s in range(NZ):
        part = ZB[s].astype(F32)
        E[pl.ds(8 * s, 8), pl.ds(0, HEADS)] = part[0:8]
        E[pl.ds(8 * s, 8), pl.ds(HEADS, HEADS)] = part[8:16]

    every = E[...]
    small = every.astype(BF16)
    contract = (((1,), (1,)), ((), ()))
    raw = lax.dot_general(small, small, contract, preferred_element_type=F32)
    cross = lax.dot_general(unit8, every, contract, precision=HIGH, preferred_element_type=F32)
    LB[mp, pl.ds(0, 32), pl.ds(0, 64)] = raw[0:32]
    LB[mp, pl.ds(0, 32), pl.ds(64, 64)] = raw[32:64]
    LB[mp, pl.ds(32, 8), pl.ds(0, 64)] = cross
    LB[mp, pl.ds(32, 8), pl.ds(64, 64)] = jnp.zeros((8, 64), F32)
    ex_send(LB, el_s, el_r)
    x_forward(1)
    x_opposite(0)
    x_send(3)
    ex_wait(LB, el_s, el_r)
    summed = LB[0]
    for s in range(1, MP):
        summed = summed + LB[s]
    logits = SHARP * jnp.concatenate([summed[0:32, 0:64], summed[0:32, 64:128]], axis=0)
    cross = summed[32:40, 0:64]

    rowi = lax.broadcasted_iota(jnp.int32, (VIEWS, VIEWS), 0)
    coli = lax.broadcasted_iota(jnp.int32, (VIEWS, VIEWS), 1)
    expo = jnp.where(rowi == coli, jnp.float32(0.0), jnp.exp(logits))
    both = expo / jnp.sum(expo, axis=1, keepdims=True) + expo / jnp.sum(expo, axis=0, keepdims=True)
    lane = lax.broadcasted_iota(jnp.int32, (1, VIEWS), 1)
    coef = []
    for v in range(2):
        index = 2 * dp + v
        mine = jnp.sum(jnp.where(rowi == index, both, 0.0), axis=0, keepdims=True)
        target = jnp.where(lane == partner_ref[index], jnp.float32(2.0), jnp.float32(0.0))
        coef.append(LOSS_MUL * (mine - target))
    r64 = lax.broadcasted_iota(jnp.int32, (8, VIEWS), 0)
    coef8 = jnp.where(r64 == 0, coef[0], jnp.where(r64 == 1, coef[1], jnp.zeros((8, VIEWS), F32)))
    demb = SHARP * jnp.dot(coef8, every, precision=HIGH, preferred_element_type=F32)
    along = SHARP * jnp.sum(coef8 * cross, axis=1, keepdims=True)
    inv8 = two(jnp.broadcast_to(squares[0], (1, BLK)), jnp.broadcast_to(squares[1], (1, BLK)), 0)
    dpooled = inv8 * (demb - unit8 * along)
    up8 = gain_ref[pl.ds(mp, 1), :] * dpooled * (1.0 / SEQ)
    UPM[mp] = jnp.zeros((8, 256), F32)
    for v in range(2):
        for c in range(3):
            UPM[mp, pl.ds(3 * v + c, 1), :] = up8[v : v + 1, 256 * c : 256 * (c + 1)]
    ex_send(UPM, eu_s, eu_r)
    x_forward(2)
    x_opposite(1)
    x_send(4)
    ex_wait(UPM, eu_s, eu_r)
    for s in range(MP):
        for v in range(2):
            for c in range(3):
                UPF[v, :, pl.ds(s * BLK + 256 * c, 256)] = UPM[s, pl.ds(3 * v + c, 1), :]

    diag = lax.broadcasted_iota(jnp.int32, (OWN, OWN), 0) == lax.broadcasted_iota(jnp.int32, (OWN, OWN), 1)
    TM[mp] = jnp.zeros((8, 128), F32)
    for v in range(2):
        acc = jnp.zeros((OWN, 128), F32)
        for q in range(D // 128):
            part = G[v, own_rows, pl.ds(q * 128, 128)].astype(F32)
            acc = acc + part * UPF[v, :, pl.ds(q * 128, 128)]
        inner = jnp.sum(acc, axis=1, keepdims=True) * (1.0 / D)
        slope = rstd[v] * rstd[v] * rstd[v] * inner
        for r, column in enumerate((rstd[v], slope)):
            line = jnp.sum(jnp.where(diag, column, 0.0), axis=0, keepdims=True)
            TM[mp, pl.ds(r, 1), pl.ds(v * OWN, OWN)] = line
    ex_send(TM, et_s, et_r)
    x_forward(3)
    x_opposite(2)
    x_send(5)
    load_ctx.wait()
    CG[...] = jnp.zeros_like(CG)
    ex_wait(TM, et_s, et_r)
    for s in range(MP):
        TT[pl.ds(8 * s, 8), :] = TM[s]
    TT[pl.ds(64, 64), :] = jnp.zeros((64, 128), F32)
    flat = TT[...].T
    for s in range(MP):
        for v in range(2):
            piece = flat[v * OWN : (v + 1) * OWN]
            RB[v, pl.ds(s * OWN, OWN), :] = jnp.broadcast_to(piece[:, 8 * s : 8 * s + 1], (OWN, 128))
            CB[v, pl.ds(s * OWN, OWN), :] = jnp.broadcast_to(piece[:, 8 * s + 1 : 8 * s + 2], (OWN, 128))

    def part_rows(dy):
        return pl.ds(pl.multiple_of(lax.rem(y + dy, NY) * PART, PART), PART)

    def half_rows(dy, h):
        start = lax.rem(y + dy, NY) * PART + h * HALF
        return pl.ds(pl.multiple_of(start, HALF), HALF)

    def ys0(k, h):
        return remote(YS0.at[k, h], YR0.at[k, h], ys0_s.at[k, h], ys0_r.at[k, h], near(dy=1 if h == 0 else -1))

    def ys1(k, h):
        return remote(YS1.at[k, h], YR1.at[k, h], ys1_s.at[k, h], ys1_r.at[k, h], near(dy=1 if h == 0 else -1))

    def zs0(h):
        return remote(ZS0.at[h], ZR0.at[h], zs0_s.at[h], zs0_r.at[h], near(dz=1 if h == 0 else -1))

    def zs1(k):
        odd = lax.rem(k, 2)
        target = lax.rem(z + NZ - 1 + 2 * odd, NZ) * NY + y
        return remote(ZS1.at[k], ZR1.at[k], zs1_s.at[k], zs1_r.at[k], (target, mp))

    def sgout(k):
        return pltpu.make_async_copy(SG.at[:, own_rows, cols(k)], sg_hbm.at[:, :, cols(k)], sgo_sem.at[k])

    def block(k):
        first = zblock(k) * BLK
        x_arrived(k)

        def build(g, carry):
            v = lax.div(g, MP)
            r = rows(lax.rem(g, MP))
            rs = RB[v, r, :]
            cs = CB[v, r, :]
            for l in range(BLK // 128):
                c = pl.ds(pl.multiple_of(first + l * 128, 128), 128)
                value = G[v, r, c].astype(F32)
                SG[v, r, c] = (rs * UPF[v, :, c] - value * cs).astype(BF16)
            return carry

        lax.fori_loop(0, 2 * MP, build, 0)
        sgout(k).start()
        keep = lax.rem(k, 3)

        left = SG[:, :, pl.ds(pl.multiple_of(first, BLK), BLK)].reshape(2 * SEQ, BLK)
        right = CTX[...].reshape(2 * SEQ, HEADS)
        PB[keep] = lax.dot_general(left, right, (((0,), (0,)), ((), ())), preferred_element_type=F32)
        for h in range(2):
            put(YS0.at[k, h], PB[keep, half_rows(2, h), :], HALF)
            ys0(k, h).start()

    def y_second(k):
        keep = lax.rem(k, 3)
        for h in range(2):
            ys0(k, h).wait_recv()
            spot = half_rows(1 if h == 0 else 3, h)
            PB[keep, spot, :] = PB[keep, spot, :] + decode(YR0.at[k, h], HALF)
            put(YS1.at[k, h], PB[keep, part_rows(1 if h == 0 else 3), :], PART)
            ys1(k, h).start()

    def z_part(k):
        keep = lax.rem(k, 3)
        ys1(k, 0).wait_recv()
        ys1(k, 1).wait_recv()
        spot = part_rows(0)
        PB[keep, spot, :] = PB[keep, spot, :] + decode(YR1.at[k, 0], PART) + decode(YR1.at[k, 1], PART)

        @pl.when(k == 0)
        def _():
            for h in range(2):
                put(ZS0.at[h], PB[keep, half_rows(0, h), :], HALF)
                zs0(h).start()

        for h in range(2):
            @pl.when(k == 1 + h)
            def _():
                zs0(h).wait_recv()
                half = half_rows(0, h)
                PB[keep, half, :] = PB[keep, half, :] + decode(ZR0.at[h], HALF)

        @pl.when(jnp.logical_and(k >= 3, k <= 6))
        def _():
            zs1(k - 2).wait_recv()
            PB[keep, spot, :] = PB[keep, spot, :] + decode(ZR1.at[k - 2], PART)

        @pl.when(jnp.logical_and(k >= 1, k <= 6))
        def _():
            put(ZS1.at[k], PB[keep, spot, :], PART)
            zs1(k).start()

        @pl.when(k == 7)
        def _():
            zs1(5).wait_recv()
            zs1(6).wait_recv()
            WGO[...] = PB[keep, spot, :] + decode(ZR1.at[5], PART) + decode(ZR1.at[6], PART)

    def project(b):
        first = zblock(b) * BLK

        left = SG[:, :, pl.ds(pl.multiple_of(first, BLK), BLK)].reshape(2 * SEQ, BLK)
        right = WT[pl.ds(pl.multiple_of(first, BLK), BLK), :]
        update = jnp.dot(left, right, preferred_element_type=F32)
        CG[...] = CG[...] + update.reshape(2, SEQ, HEADS)

    def iteration(k, carry):
        @pl.when(k <= 1)
        def _():
            x_send(k + 6)

        @pl.when(k <= 3)
        def _():
            x_forward(k + 4)

        @pl.when(k <= 4)
        def _():
            x_opposite(k + 3)

        for f in range(1, 4):
            @pl.when(k == 2 * f - 2)
            def _():
                wz_next(f)

        @pl.when(k <= 7)
        def _():
            block(k)

        @pl.when(jnp.logical_and(k >= 1, k <= 8))
        def _():
            y_second(k - 1)

        @pl.when(k >= 2)
        def _():
            z_part(k - 2)

        @pl.when(jnp.logical_and(k >= 4, k <= 5))
        def _():
            project(k - 1)

        @pl.when(jnp.logical_and(k >= 6, k <= 7))
        def _():
            project(k - 5)

        @pl.when(k == 8)
        def _():
            project(5)
            project(6)
            project(7)
            wz_wait(3, 0)
            wz_wait(3, 1)
            project(0)
            CGO[...] = CG[...].astype(BF16)
            pltpu.make_async_copy(CGO, cg_hbm, out_sem.at[0]).start()

        return carry

    lax.fori_loop(0, 10, iteration, 0)
    wg_out = pltpu.make_async_copy(WGO, wg_hbm, out_sem.at[1])
    wg_out.start()

    def drain(k, carry):
        for t in range(3):
            x_own(k, t).wait_send()
            x_sib(k, t).wait_send()
        for h in range(2):
            x_fwd(k, h).wait_send()
            ys0(k, h).wait_send()
            ys1(k, h).wait_send()
        sgout(k).wait()

        @pl.when(jnp.logical_and(k >= 1, k <= 6))
        def _():
            zs1(k).wait_send()

        return carry

    lax.fori_loop(0, NZ, drain, 0)
    for h in range(2):
        zs0(h).wait_send()
    for d in range(1, NY):
        wy_copy(d).wait_send()
        ey_copy(d).wait_send()
    for f in range(4):
        for t in range(2):
            wz_copy(f, t).wait_send()
    for d in range(1, NZ):
        ez_copy(d).wait_send()
    for d in range(1, MP):
        ex(EX1, e1_s, e1_r, d).wait_send()
        ex(LB, el_s, el_r, d).wait_send()
        ex(UPM, eu_s, eu_r, d).wait_send()
        ex(TM, et_s, et_r, d).wait_send()
    pltpu.make_async_copy(CGO, cg_hbm, out_sem.at[0]).wait()
    wg_out.wait()


def copy_out(cg, wg, sg, cg_out, wg_out, sg_out, sem):
    copies = [pltpu.make_async_copy(sg.at[v], sg_out.at[v], sem.at[v]) for v in range(2)]
    copies += [pltpu.make_async_copy(cg.at[v], cg_out.at[v], sem.at[2 + v]) for v in range(2)]
    copies.append(pltpu.make_async_copy(wg, wg_out, sem.at[4]))
    for c in copies:
        c.start()
    for c in copies:
        c.wait()


def local(context, w_out, stream, gain, partner):
    anywhere = pl.BlockSpec(memory_space=pl.ANY)
    sems = pltpu.SemaphoreType.DMA
    vm = pltpu.VMEM
    scratch = [
        vm((2, SEQ, D), BF16), vm((2, SEQ, D), BF16), vm((D, HEADS), BF16), vm((2, SEQ, HEADS), BF16),
        vm((2, SEQ, HEADS), F32), vm((2, SEQ, HEADS), BF16), vm((3, BLK, HEADS), F32), vm((PART, HEADS), F32),
        vm((MP, 2, MP, BLK), F32), vm((2, MP, BLK), F32), vm((NY, 8, BLK), F32), vm((NZ, 16, HEADS), BF16),
        vm((VIEWS, BLK), F32), vm((MP, 40, 128), F32), vm((MP, 8, 256), F32), vm((2, 1, D), F32),
        vm((MP, 8, 128), F32), vm((128, 128), F32), vm((2, SEQ, 128), F32), vm((2, SEQ, 128), F32),
        vm((NZ, 2, PAYH, HEADS), I16), vm((NZ, 2, PAYH, HEADS), I16),
        vm((NZ, 2, PAY, HEADS), I16), vm((NZ, 2, PAY, HEADS), I16),
        vm((2, PAYH, HEADS), I16), vm((2, PAYH, HEADS), I16),
        vm((NZ, PAY, HEADS), I16), vm((NZ, PAY, HEADS), I16),
        sems((3,)), sems((2,)), sems((NZ,)),
        sems((NZ, 8)), sems((NZ, 8)), sems((NY - 1,)), sems((NY,)), sems((4, 2)), sems((4, 2)),
        sems((MP - 1,)), sems((MP,)), sems((NY - 1,)), sems((NY,)), sems((NZ - 1,)), sems((NZ,)),
        sems((MP - 1,)), sems((MP,)), sems((MP - 1,)), sems((MP,)), sems((MP - 1,)), sems((MP,)),
        sems((NZ, 2)), sems((NZ, 2)), sems((NZ, 2)), sems((NZ, 2)),
        sems((2,)), sems((2,)), sems((NZ,)), sems((NZ,)),
    ]
    context_grad, weight_grad, stream_grad = pl.pallas_call(
        kernel,
        out_shape=(
            jax.ShapeDtypeStruct(context.shape, BF16),
            jax.ShapeDtypeStruct((PART, HEADS), F32),
            jax.ShapeDtypeStruct(stream.shape, BF16),
        ),
        in_specs=[
            anywhere, anywhere, anywhere,
            pl.BlockSpec(memory_space=pltpu.VMEM),
            pl.BlockSpec(memory_space=pltpu.SMEM),
        ],
        out_specs=[anywhere] * 3,
        scratch_shapes=scratch,
        compiler_params=pltpu.CompilerParams(
            collective_id=0, has_side_effects=True, vmem_limit_bytes=60 * 2**20
        ),
        cost_estimate=pl.CostEstimate(flops=10**10, bytes_accessed=6 * 10**6, transcendentals=0),
    )(context, w_out.T, stream, gain.reshape(MP, BLK), partner)
    context_grad, weight_grad, stream_grad = pl.pallas_call(
        copy_out,
        out_shape=tuple(jax.ShapeDtypeStruct(a.shape, a.dtype) for a in (context_grad, weight_grad, stream_grad)),
        in_specs=[anywhere] * 3,
        out_specs=[anywhere] * 3,
        scratch_shapes=[sems((5,))],
    )(context_grad, weight_grad, stream_grad)
    return context_grad, weight_grad.T, stream_grad


def solution(mesh):
    placed = (P("dp", None, "mp"), P("mp", "dp"), P("dp", "mp", None), P(), P())
    return jax.shard_map(
        local,
        mesh=mesh,
        in_specs=placed,
        out_specs=(P("dp", None, "mp"), P("mp", "dp"), P("dp", "mp", None)),
        check_vma=False,
    )
```

```python
import jax
import jax.numpy as jnp
from jax import lax
from jax.experimental import pallas as pl
from jax.experimental.pallas import tpu as pltpu
from jax.sharding import PartitionSpec as P

EPS = 1e-06
SHARP = 10.0
LOSS_MUL = 512.0
D = 6144
SEQ = 512
HEADS = 384
VIEWS = 64
NZ, NY, NX = 8, 4, 4
MP = 8
OWN = 64
BLK = 768
PART = 192
HALF = PART // 2
PAY = PART + 16
PAYH = HALF + 16
WIDE = 256
THIN = HEADS - WIDE
F32 = jnp.float32
BF16 = jnp.bfloat16
I16 = jnp.int16
HIGH = lax.Precision.HIGHEST


def encode(values):
    top = jnp.max(jnp.abs(values), axis=0, keepdims=True)
    expo = jnp.ceil(16.0 * jnp.log2(jnp.maximum(top, 1e-30)))
    whole = jnp.round(values * jnp.exp2(14.9 - expo * 0.0625)).astype(jnp.int32).astype(I16)
    tail = jnp.broadcast_to(expo, (16, values.shape[1])).astype(jnp.int32).astype(I16)
    return whole, tail


def decode(ref, rows):
    expo = ref[pl.ds(rows, 16), :].astype(jnp.int32).astype(F32)[0:1, :]
    return ref[pl.ds(0, rows), :].astype(jnp.int32).astype(F32) * jnp.exp2(expo * 0.0625 - 14.9)


def put(ref, values, rows):
    whole, tail = encode(values)
    ref[pl.ds(0, rows), :] = whole
    ref[pl.ds(rows, 16), :] = tail


def kernel(
    ctx_hbm, w_hbm, stream_hbm, gain_ref, partner_ref,
    cg_hbm, wg_hbm, sg_hbm,
    G, SG, WT, CTX, CG, CGO, PB, WGO,
    EX1, UN, YB, ZB, E, LB, UPM, UPF, TM, TT, RB, CB,
    YS0, YR0, YS1, YR1, ZS0, ZR0, ZS1, ZR1,
    BZS0, BZR0, BZS1, BZR1, BYS0, BYR0, BYS1, BYR1,
    in_sem, out_sem, sgo_sem,
    xs_s, x_r, wy_s, wy_r, wz_s, wz_r,
    e1_s, e1_r, ey_s, ey_r, ez_s, ez_r, el_s, el_r, eu_s, eu_r, et_s, et_r,
    ys0_s, ys0_r, ys1_s, ys1_r, zs0_s, zs0_r, zs1_s, zs1_r,
    bz0_s, bz0_r, bz1_s, bz1_r, by0_s, by0_r, by1_s, by1_r,
    vz_s, vz_r, vw_s, vw_r, vy_s, vy_r,
):
    dp = lax.axis_index("dp")
    mp = lax.axis_index("mp")
    z, y = lax.div(dp, NY), lax.rem(dp, NY)
    x, core = lax.div(mp, 2), lax.rem(mp, 2)

    def zy(dz, dy):
        return lax.rem(z + (dz + NZ), NZ) * NY + lax.rem(y + (dy + NY), NY)

    def slot(dx, other):
        c = 1 - core if other else core
        return lax.rem(x + (dx + NX), NX) * 2 + c

    def near(dx=0, other=False, dz=0, dy=0):
        return (zy(dz, dy), slot(dx, other))

    def remote(src, dst, ss, rs, dev):
        return pltpu.make_async_remote_copy(
            src_ref=src, dst_ref=dst, send_sem=ss, recv_sem=rs,
            device_id=dev, device_id_type=pl.DeviceIdType.MESH,
        )

    own_rows = pl.ds(pl.multiple_of(mp * OWN, OWN), OWN)
    load_stream = pltpu.make_async_copy(stream_hbm, G.at[:, own_rows, :], in_sem.at[0])
    load_ctx = pltpu.make_async_copy(ctx_hbm, CTX, in_sem.at[1])
    load_w = pltpu.make_async_copy(
        w_hbm, WT.at[z, y], in_sem.at[2]
    )
    load_stream.start()
    load_w.start()
    load_ctx.start()

    barrier = pltpu.get_barrier_semaphore()
    peers = [(dp, lax.rem(mp + d, MP)) for d in range(1, MP)]
    ypeers = [near(dy=d) for d in range(1, NY)]
    zpeers = [near(dz=d) for d in range(1, NZ)]
    for dev in peers + ypeers + zpeers:
        pl.semaphore_signal(barrier, inc=1, device_id=dev, device_id_type=pl.DeviceIdType.MESH)

    def zblock(k):
        dist = lax.div(NZ - k, 2)
        odd = lax.rem(k, 2)
        return lax.rem(z + NZ + (2 * odd - 1) * dist, NZ)

    def cols(k):
        return pl.ds(pl.multiple_of(zblock(k) * BLK, BLK), BLK)

    def rows(s):
        return pl.ds(pl.multiple_of(s * OWN, OWN), OWN)

    def x_own(k, t):
        ref = G.at[:, own_rows, cols(k)]
        dev = (near(dx=1), near(dx=-1), near(other=True))[t]
        return remote(ref, ref, xs_s.at[k, t], x_r.at[k, t], dev)

    def x_fwd(k, t):
        if t == 0:
            ref = G.at[0, rows(slot(-1, False)), cols(k)]
            return remote(ref, ref, xs_s.at[k, 3], x_r.at[k, 3], near(dx=1))
        ref = G.at[1, rows(slot(1, False)), cols(k)]
        return remote(ref, ref, xs_s.at[k, 4], x_r.at[k, 4], near(dx=-1))

    def x_sib(k, t):
        ref = G.at[:, rows(slot((-1, 1, 2)[t], False)), cols(k)]
        return remote(ref, ref, xs_s.at[k, 5 + t], x_r.at[k, 5 + t], near(other=True))

    def x_wait(k, t):
        if t < 3:
            ref = G.at[:, rows((slot(-1, False), slot(1, False), slot(0, True))[t]), cols(k)]
        elif t < 5:
            ref = G.at[t - 3, rows(slot(2, False)), cols(k)]
        else:
            ref = G.at[:, rows(slot((-1, 1, 2)[t - 5], True)), cols(k)]
        remote(ref, ref, xs_s.at[k, t], x_r.at[k, t], near(other=True)).wait_recv()

    def x_send(k):
        for t in range(3):
            x_own(k, t).start()

    def x_forward(k):
        x_wait(k, 0)
        x_fwd(k, 0).start()
        x_sib(k, 0).start()
        x_wait(k, 1)
        x_fwd(k, 1).start()
        x_sib(k, 1).start()

    def x_opposite(k):
        x_wait(k, 3)
        x_wait(k, 4)
        x_sib(k, 2).start()

    def x_arrived(k):
        x_wait(k, 2)
        for t in (5, 6, 7):
            x_wait(k, t)

    def wy_copy(d):
        ref = WT.at[z, y, pl.ds(0, HALF), :]
        return remote(ref, ref, wy_s.at[d - 1], wy_r.at[y], near(dy=d))

    def wy_wait(d):
        s = lax.rem(y + d, NY)
        ref = WT.at[z, s, pl.ds(0, HALF), :]
        remote(ref, ref, wy_s.at[d - 1], wy_r.at[s], near(dy=d)).wait_recv()

    def wz_ref(bundle, f, t):
        if f == 3:
            return WT.at[bundle, pl.ds(2 * t, 2), pl.ds(0, HALF), :]
        return WT.at[bundle, :, pl.ds(0, HALF), :]

    def wz_copy(f, t):
        step = f if t else NZ - f
        ref = wz_ref(lax.rem(z + step, NZ), f, t)
        return remote(ref, ref, wz_s.at[f, t], wz_r.at[f, t], near(dz=-1 if t else 1))

    def wz_wait(f, t):
        step = f + 1 if t else NZ - f - 1
        ref = wz_ref(lax.rem(z + step, NZ), f, t)
        remote(ref, ref, wz_s.at[f, t], wz_r.at[f, t], near(dz=1)).wait_recv()

    def vz_ref(bundle, f, t):
        if f == 3:
            return WT.at[bundle, y, pl.ds(HALF + t * (HALF // 2), HALF // 2), :]
        return WT.at[bundle, y, pl.ds(HALF, HALF), :]

    def vz_copy(f, t):
        step = f if t else NZ - f
        ref = vz_ref(lax.rem(z + step, NZ), f, t)
        return remote(ref, ref, vz_s.at[f, t], vz_r.at[f, t], near(dz=-1 if t else 1))

    def vz_wait(f, t):
        step = f + 1 if t else NZ - f - 1
        ref = vz_ref(lax.rem(z + step, NZ), f, t)
        remote(ref, ref, vz_s.at[f, t], vz_r.at[f, t], near(dz=1)).wait_recv()

    def vw_ref(n, dy):
        return WT.at[lax.rem(z + NZ - n, NZ), lax.rem(y + NY + dy, NY), pl.ds(HALF, HALF), :]

    def vw_copy(n, t):
        ref = vw_ref(n, 0)
        return remote(ref, ref, vw_s.at[n, t], vw_r.at[n, t], near(dy=-1 if t else 1))

    def vw_wait(n, t):
        ref = vw_ref(n, 1 if t else -1)
        remote(ref, ref, vw_s.at[n, t], vw_r.at[n, t], near(dy=1)).wait_recv()

    def vw_send(n):
        for t in range(2):
            vw_copy(n, t).start()

    def vz_next(f):
        for t in range(2):
            vz_wait(f - 1, t)
            vz_copy(f, t).start()
            vw_send(NZ - f if t else f)

    def vy_ref(dy, part):
        s = lax.rem(y + NY + dy, NY)
        return WT.at[pl.ds(part * (NZ // 2), NZ // 2), s, pl.ds(HALF, HALF), :]

    def vy_copy(t):
        ref = vy_ref(1 if t else -1, t)
        return remote(ref, ref, vy_s.at[t], vy_r.at[t], near(dy=-1 if t else 1))

    def vy_wait(t):
        ref = vy_ref(2, t)
        remote(ref, ref, vy_s.at[t], vy_r.at[t], near(dy=1)).wait_recv()

    def vy_begin():
        for t in range(2):
            vz_wait(3, t)
        vw_send(NZ // 2)

    def vy_next():
        for t in range(2):
            for n in range(NZ):
                vw_wait(n, t)
            vy_copy(t).start()

    def wz_next(f):
        for t in range(2):
            wz_wait(f - 1, t)
            wz_copy(f, t).start()

    def ex(buf, ss, rs, d):
        ref = buf.at[mp]
        return remote(ref, ref, ss.at[d - 1], rs.at[mp], (dp, lax.rem(mp + d, MP)))

    def ex_send(buf, ss, rs):
        for d in (4, 2, 3, 5, 6, 7, 1):
            ex(buf, ss, rs, d).start()

    def ex_wait(buf, ss, rs):
        for d in range(1, MP):
            s = lax.rem(mp + d, MP)
            ref = buf.at[s]
            remote(ref, ref, ss.at[d - 1], rs.at[s], (dp, s)).wait_recv()

    def ey_copy(d):
        ref = YB.at[y]
        return remote(ref, ref, ey_s.at[d - 1], ey_r.at[y], near(dy=d))

    def ez_copy(d):
        ref = ZB.at[z]
        return remote(ref, ref, ez_s.at[d - 1], ez_r.at[z], near(dz=d))

    load_stream.wait()

    def rstd_of(v):
        acc = jnp.zeros((OWN, 128), F32)
        for q in range(D // 128):
            part = G[v, own_rows, pl.ds(q * 128, 128)].astype(F32)
            acc = acc + part * part
        mean = jnp.sum(acc, axis=1, keepdims=True) * (1.0 / D)
        return lax.rsqrt(mean + EPS)

    rstd = [rstd_of(v) for v in range(2)]
    for v in range(2):
        for q in range(MP):
            part = G[v, own_rows, pl.ds(q * BLK, BLK)].astype(F32)
            EX1[mp, v, pl.ds(q, 1), :] = jnp.sum(part * rstd[v], axis=0, keepdims=True)

    pl.semaphore_wait(barrier, (MP - 1) + (NY - 1) + (NZ - 1))
    ex_send(EX1, e1_s, e1_r)
    load_w.wait()
    for d in (2, 1, 3):
        wy_copy(d).start()
    for t in range(2):
        vz_copy(0, t).start()
    vw_send(0)
    x_send(0)
    x_send(1)
    ex_wait(EX1, e1_s, e1_r)

    gain8 = gain_ref[...]
    squares = []
    for v in range(2):
        total = EX1[0, v]
        for s in range(1, MP):
            total = total + EX1[s, v]
        pooled = total * gain8 * (1.0 / SEQ)
        UN[v] = pooled
        sq = jnp.sum(jnp.sum(pooled * pooled, axis=1, keepdims=True), axis=0, keepdims=True)
        squares.append(lax.rsqrt(sq + EPS))
    unit = [UN[v, pl.ds(mp, 1), :] * squares[v] for v in range(2)]
    emb = [u.astype(BF16).astype(F32) for u in unit]
    row8 = lax.broadcasted_iota(jnp.int32, (8, BLK), 0)
    zero8 = jnp.zeros((8, BLK), F32)

    def two(a, b, first):
        return jnp.where(row8 == first, a, jnp.where(row8 == first + 1, b, zero8))

    YB[y] = two(emb[0], emb[1], 2 * y)
    for d in (2, 1, 3):
        ey_copy(d).start()
    unit8 = two(unit[0], unit[1], 0)
    for d in range(1, NY):
        s = lax.rem(y + d, NY)
        ref = YB.at[s]
        remote(ref, ref, ey_s.at[d - 1], ey_r.at[s], near(dy=d)).wait_recv()
    eight = YB[0] + YB[1] + YB[2] + YB[3]
    ZB[z] = jnp.concatenate([eight[:, 0:HEADS], eight[:, HEADS:BLK]], axis=0).astype(BF16)
    for d in (4, 3, 5, 2, 6, 1, 7):
        ez_copy(d).start()
    vz_next(1)
    for d in range(1, NY):
        wy_wait(d)
    for t in range(2):
        wz_copy(0, t).start()
    x_forward(0)
    x_send(2)
    for d in range(1, NZ):
        s = lax.rem(z + d, NZ)
        ref = ZB.at[s]
        remote(ref, ref, ez_s.at[d - 1], ez_r.at[s], near(dz=d)).wait_recv()
    for s in range(NZ):
        part = ZB[s].astype(F32)
        E[pl.ds(8 * s, 8), pl.ds(0, HEADS)] = part[0:8]
        E[pl.ds(8 * s, 8), pl.ds(HEADS, HEADS)] = part[8:16]

    every = E[...]
    small = every.astype(BF16)
    contract = (((1,), (1,)), ((), ()))
    raw = lax.dot_general(small, small, contract, preferred_element_type=F32)
    cross = lax.dot_general(unit8, every, contract, precision=HIGH, preferred_element_type=F32)
    LB[mp, pl.ds(0, 32), pl.ds(0, 64)] = raw[0:32]
    LB[mp, pl.ds(0, 32), pl.ds(64, 64)] = raw[32:64]
    LB[mp, pl.ds(32, 8), pl.ds(0, 64)] = cross
    LB[mp, pl.ds(32, 8), pl.ds(64, 64)] = jnp.zeros((8, 64), F32)
    ex_send(LB, el_s, el_r)
    vz_next(2)
    wz_next(1)
    x_forward(1)
    x_opposite(0)
    x_send(3)
    ex_wait(LB, el_s, el_r)
    summed = LB[0]
    for s in range(1, MP):
        summed = summed + LB[s]
    logits = SHARP * jnp.concatenate([summed[0:32, 0:64], summed[0:32, 64:128]], axis=0)
    cross = summed[32:40, 0:64]

    rowi = lax.broadcasted_iota(jnp.int32, (VIEWS, VIEWS), 0)
    coli = lax.broadcasted_iota(jnp.int32, (VIEWS, VIEWS), 1)
    expo = jnp.where(rowi == coli, jnp.float32(0.0), jnp.exp(logits))
    both = expo / jnp.sum(expo, axis=1, keepdims=True) + expo / jnp.sum(expo, axis=0, keepdims=True)
    lane = lax.broadcasted_iota(jnp.int32, (1, VIEWS), 1)
    coef = []
    for v in range(2):
        index = 2 * dp + v
        mine = jnp.sum(jnp.where(rowi == index, both, 0.0), axis=0, keepdims=True)
        target = jnp.where(lane == partner_ref[index], jnp.float32(2.0), jnp.float32(0.0))
        coef.append(LOSS_MUL * (mine - target))
    r64 = lax.broadcasted_iota(jnp.int32, (8, VIEWS), 0)
    coef8 = jnp.where(r64 == 0, coef[0], jnp.where(r64 == 1, coef[1], jnp.zeros((8, VIEWS), F32)))
    demb = SHARP * jnp.dot(coef8, every, precision=HIGH, preferred_element_type=F32)
    along = SHARP * jnp.sum(coef8 * cross, axis=1, keepdims=True)
    inv8 = two(jnp.broadcast_to(squares[0], (1, BLK)), jnp.broadcast_to(squares[1], (1, BLK)), 0)
    dpooled = inv8 * (demb - unit8 * along)
    up8 = gain_ref[pl.ds(mp, 1), :] * dpooled * (1.0 / SEQ)
    UPM[mp] = jnp.zeros((8, 256), F32)
    for v in range(2):
        for c in range(3):
            UPM[mp, pl.ds(3 * v + c, 1), :] = up8[v : v + 1, 256 * c : 256 * (c + 1)]
    ex_send(UPM, eu_s, eu_r)
    x_forward(2)
    x_opposite(1)
    x_send(4)
    vz_next(3)
    ex_wait(UPM, eu_s, eu_r)
    for s in range(MP):
        for v in range(2):
            for c in range(3):
                UPF[v, :, pl.ds(s * BLK + 256 * c, 256)] = UPM[s, pl.ds(3 * v + c, 1), :]

    diag = lax.broadcasted_iota(jnp.int32, (OWN, OWN), 0) == lax.broadcasted_iota(jnp.int32, (OWN, OWN), 1)
    TM[mp] = jnp.zeros((8, 128), F32)
    for v in range(2):
        acc = jnp.zeros((OWN, 128), F32)
        for q in range(D // 128):
            part = G[v, own_rows, pl.ds(q * 128, 128)].astype(F32)
            acc = acc + part * UPF[v, :, pl.ds(q * 128, 128)]
        inner = jnp.sum(acc, axis=1, keepdims=True) * (1.0 / D)
        slope = rstd[v] * rstd[v] * rstd[v] * inner
        for r, column in enumerate((rstd[v], slope)):
            line = jnp.sum(jnp.where(diag, column, 0.0), axis=0, keepdims=True)
            TM[mp, pl.ds(r, 1), pl.ds(v * OWN, OWN)] = line
    ex_send(TM, et_s, et_r)
    vy_begin()
    wz_next(2)
    x_forward(3)
    x_opposite(2)
    x_send(5)
    load_ctx.wait()
    CG[...] = jnp.zeros_like(CG)
    ex_wait(TM, et_s, et_r)
    for s in range(MP):
        TT[pl.ds(8 * s, 8), :] = TM[s]
    TT[pl.ds(64, 64), :] = jnp.zeros((64, 128), F32)
    flat = TT[...].T
    for s in range(MP):
        for v in range(2):
            piece = flat[v * OWN : (v + 1) * OWN]
            RB[v, pl.ds(s * OWN, OWN), :] = jnp.broadcast_to(piece[:, 8 * s : 8 * s + 1], (OWN, 128))
            CB[v, pl.ds(s * OWN, OWN), :] = jnp.broadcast_to(piece[:, 8 * s + 1 : 8 * s + 2], (OWN, 128))

    wide, thin = pl.ds(0, WIDE), pl.ds(WIDE, THIN)

    def part_rows(dy):
        return pl.ds(pl.multiple_of(lax.rem(y + dy, NY) * PART, PART), PART)

    def half_rows(dy, h):
        start = lax.rem(y + dy, NY) * PART + h * HALF
        return pl.ds(pl.multiple_of(start, HALF), HALF)

    def ys0(k, h):
        return remote(YS0.at[k, h], YR0.at[k, h], ys0_s.at[k, h], ys0_r.at[k, h], near(dy=1 if h == 0 else -1))

    def ys1(k, h):
        return remote(YS1.at[k, h], YR1.at[k, h], ys1_s.at[k, h], ys1_r.at[k, h], near(dy=1 if h == 0 else -1))

    def zs0(h):
        return remote(ZS0.at[h], ZR0.at[h], zs0_s.at[h], zs0_r.at[h], near(dz=1 if h == 0 else -1))

    def zs1(k):
        odd = lax.rem(k, 2)
        target = lax.rem(z + NZ - 1 + 2 * odd, NZ) * NY + y
        return remote(ZS1.at[k], ZR1.at[k], zs1_s.at[k], zs1_r.at[k], (target, mp))

    def sgout(k):
        return pltpu.make_async_copy(SG.at[:, own_rows, cols(k)], sg_hbm.at[:, :, cols(k)], sgo_sem.at[k])

    def block(k):
        first = zblock(k) * BLK
        x_arrived(k)

        def build(g, carry):
            v = lax.div(g, MP)
            r = rows(lax.rem(g, MP))
            rs = RB[v, r, :]
            cs = CB[v, r, :]
            for l in range(BLK // 128):
                c = pl.ds(pl.multiple_of(first + l * 128, 128), 128)
                value = G[v, r, c].astype(F32)
                SG[v, r, c] = (rs * UPF[v, :, c] - value * cs).astype(BF16)
            return carry

        lax.fori_loop(0, 2 * MP, build, 0)
        sgout(k).start()
        keep = lax.rem(k, 5)

        left = SG[:, :, pl.ds(pl.multiple_of(first, BLK), BLK)].reshape(2 * SEQ, BLK)
        right = CTX[...].reshape(2 * SEQ, HEADS)
        PB[keep] = lax.dot_general(left, right, (((0,), (0,)), ((), ())), preferred_element_type=F32)
        for h in range(2):
            put(YS0.at[k, h], PB[keep, half_rows(2, h), wide], HALF)
            ys0(k, h).start()

    def y_second(k):
        keep = lax.rem(k, 5)
        for h in range(2):
            ys0(k, h).wait_recv()
            spot = half_rows(1 if h == 0 else 3, h)
            PB[keep, spot, wide] = PB[keep, spot, wide] + decode(YR0.at[k, h], HALF)
            put(YS1.at[k, h], PB[keep, part_rows(1 if h == 0 else 3), wide], PART)
            ys1(k, h).start()

    def z_part(k):
        keep = lax.rem(k, 5)
        ys1(k, 0).wait_recv()
        ys1(k, 1).wait_recv()
        spot = part_rows(0)
        PB[keep, spot, wide] = PB[keep, spot, wide] + decode(YR1.at[k, 0], PART) + decode(YR1.at[k, 1], PART)

        @pl.when(k == 0)
        def _():
            for h in range(2):
                put(ZS0.at[h], PB[keep, half_rows(0, h), wide], HALF)
                zs0(h).start()

        for h in range(2):
            @pl.when(k == 1 + h)
            def _():
                zs0(h).wait_recv()
                half = half_rows(0, h)
                PB[keep, half, wide] = PB[keep, half, wide] + decode(ZR0.at[h], HALF)

        @pl.when(jnp.logical_and(k >= 3, k <= 6))
        def _():
            zs1(k - 2).wait_recv()
            PB[keep, spot, wide] = PB[keep, spot, wide] + decode(ZR1.at[k - 2], PART)

        @pl.when(jnp.logical_and(k >= 1, k <= 6))
        def _():
            put(ZS1.at[k], PB[keep, spot, wide], PART)
            zs1(k).start()

        @pl.when(k == 7)
        def _():
            zs1(5).wait_recv()
            zs1(6).wait_recv()
            WGO[:, wide] = PB[keep, spot, wide] + decode(ZR1.at[5], PART) + decode(ZR1.at[6], PART)

    def bz0(h):
        return remote(BZS0.at[h], BZR0.at[h], bz0_s.at[h], bz0_r.at[h], near(dz=1 if h == 0 else -1))

    def bz1(k):
        odd = lax.rem(k, 2)
        target = lax.rem(z + NZ - 1 + 2 * odd, NZ) * NY + y
        return remote(BZS1.at[k], BZR1.at[k], bz1_s.at[k], bz1_r.at[k], (target, mp))

    def by0(h):
        return remote(BYS0.at[h], BYR0.at[h], by0_s.at[h], by0_r.at[h], near(dy=1 if h == 0 else -1))

    def by1(h):
        return remote(BYS1.at[h], BYR1.at[h], by1_s.at[h], by1_r.at[h], near(dy=1 if h == 0 else -1))

    def b_part(k):
        keep = lax.rem(k, 5)

        @pl.when(k == 0)
        def _():
            for h in range(2):
                put(BZS0.at[h], PB[keep, pl.ds(h * BLK // 2, BLK // 2), thin], BLK // 2)
                bz0(h).start()

        for h in range(2):
            @pl.when(k == 1 + h)
            def _():
                bz0(h).wait_recv()
                half = pl.ds(h * BLK // 2, BLK // 2)
                PB[keep, half, thin] = PB[keep, half, thin] + decode(BZR0.at[h], BLK // 2)

        @pl.when(jnp.logical_and(k >= 3, k <= 6))
        def _():
            bz1(k - 2).wait_recv()
            PB[keep, :, thin] = PB[keep, :, thin] + decode(BZR1.at[k - 2], BLK)

        @pl.when(jnp.logical_and(k >= 1, k <= 6))
        def _():
            put(BZS1.at[k], PB[keep, :, thin], BLK)
            bz1(k).start()

        @pl.when(k == 7)
        def _():
            bz1(5).wait_recv()
            bz1(6).wait_recv()
            PB[keep, :, thin] = PB[keep, :, thin] + decode(BZR1.at[5], BLK) + decode(BZR1.at[6], BLK)
            for h in range(2):
                put(BYS0.at[h], PB[keep, half_rows(2, h), thin], HALF)
                by0(h).start()

    def b_second():
        for h in range(2):
            by0(h).wait_recv()
            spot = half_rows(1 if h == 0 else 3, h)
            PB[2, spot, thin] = PB[2, spot, thin] + decode(BYR0.at[h], HALF)
            put(BYS1.at[h], PB[2, part_rows(1 if h == 0 else 3), thin], PART)
            by1(h).start()

    def b_last():
        by1(0).wait_recv()
        by1(1).wait_recv()
        WGO[:, thin] = PB[2, part_rows(0), thin] + decode(BYR1.at[0], PART) + decode(BYR1.at[1], PART)

    def project(b):
        first = zblock(b) * BLK

        left = SG[:, :, pl.ds(pl.multiple_of(first, BLK), BLK)].reshape(2 * SEQ, BLK)
        right = WT[zblock(b)].reshape(BLK, HEADS)
        update = jnp.dot(left, right, preferred_element_type=F32)
        CG[...] = CG[...] + update.reshape(2, SEQ, HEADS)

    def iteration(k, carry):
        @pl.when(k <= 1)
        def _():
            x_send(k + 6)

        @pl.when(k <= 3)
        def _():
            x_forward(k + 4)

        @pl.when(k <= 4)
        def _():
            x_opposite(k + 3)

        @pl.when(k == 1)
        def _():
            wz_next(3)

        @pl.when(k == 0)
        def _():
            vy_next()

        @pl.when(k == 4)
        def _():
            for t in range(2):
                wz_wait(3, t)
                vy_wait(t)

        @pl.when(k <= 7)
        def _():
            block(k)

        @pl.when(jnp.logical_and(k >= 1, k <= 8))
        def _():
            b_part(k - 1)

        @pl.when(jnp.logical_and(k >= 2, k <= 9))
        def _():
            y_second(k - 2)

        @pl.when(k >= 4)
        def _():
            z_part(k - 4)

        @pl.when(jnp.logical_and(k >= 4, k <= 5))
        def _():
            project(k - 1)

        @pl.when(jnp.logical_and(k >= 6, k <= 7))
        def _():
            project(k - 5)

        @pl.when(k == 8)
        def _():
            project(5)
            project(6)

        @pl.when(k == 9)
        def _():
            b_second()
            project(7)
            project(0)
            CGO[...] = CG[...].astype(BF16)
            pltpu.make_async_copy(CGO, cg_hbm, out_sem.at[0]).start()

        return carry

    lax.fori_loop(0, 12, iteration, 0)
    b_last()
    wg_out = pltpu.make_async_copy(WGO, wg_hbm, out_sem.at[1])
    wg_out.start()

    def drain(k, carry):
        for t in range(3):
            x_own(k, t).wait_send()
            x_sib(k, t).wait_send()
        for h in range(2):
            x_fwd(k, h).wait_send()
            ys0(k, h).wait_send()
            ys1(k, h).wait_send()
        sgout(k).wait()

        @pl.when(jnp.logical_and(k >= 1, k <= 6))
        def _():
            zs1(k).wait_send()
            bz1(k).wait_send()

        return carry

    lax.fori_loop(0, NZ, drain, 0)
    for h in range(2):
        zs0(h).wait_send()
        bz0(h).wait_send()
        by0(h).wait_send()
        by1(h).wait_send()
        vy_copy(h).wait_send()
        for n in range(NZ):
            vw_copy(n, h).wait_send()
    for d in range(1, NY):
        wy_copy(d).wait_send()
        ey_copy(d).wait_send()
    for f in range(4):
        for t in range(2):
            wz_copy(f, t).wait_send()
            vz_copy(f, t).wait_send()
    for d in range(1, NZ):
        ez_copy(d).wait_send()
    for d in range(1, MP):
        ex(EX1, e1_s, e1_r, d).wait_send()
        ex(LB, el_s, el_r, d).wait_send()
        ex(UPM, eu_s, eu_r, d).wait_send()
        ex(TM, et_s, et_r, d).wait_send()
    pltpu.make_async_copy(CGO, cg_hbm, out_sem.at[0]).wait()
    wg_out.wait()


def copy_out(cg, wg, sg, cg_out, wg_out, sg_out, cg_mid, wg_mid, sg_mid, sem_in, sem_out):
    moves = [(sg, sg_mid, sg_out, v) for v in range(2)] + [(cg, cg_mid, cg_out, v) for v in range(2)]
    moves = [(a.at[v], b.at[v], c.at[v]) for a, b, c, v in moves] + [(wg, wg_mid, wg_out)]
    loads = [pltpu.make_async_copy(a, b, sem_in.at[n]) for n, (a, b, c) in enumerate(moves)]
    stores = [pltpu.make_async_copy(b, c, sem_out.at[n]) for n, (a, b, c) in enumerate(moves)]
    for load in loads:
        load.start()
    for load, store in zip(loads, stores):
        load.wait()
        store.start()
    for store in stores:
        store.wait()


def local(context, w_out, stream, gain, partner):
    anywhere = pl.BlockSpec(memory_space=pl.ANY)
    sems = pltpu.SemaphoreType.DMA
    vm = pltpu.VMEM
    scratch = [
        vm((2, SEQ, D), BF16), vm((2, SEQ, D), BF16), vm((NZ, NY, PART, HEADS), BF16), vm((2, SEQ, HEADS), BF16),
        vm((2, SEQ, HEADS), F32), vm((2, SEQ, HEADS), BF16), vm((5, BLK, HEADS), F32), vm((PART, HEADS), F32),
        vm((MP, 2, MP, BLK), F32), vm((2, MP, BLK), F32), vm((NY, 8, BLK), F32), vm((NZ, 16, HEADS), BF16),
        vm((VIEWS, BLK), F32), vm((MP, 40, 128), F32), vm((MP, 8, 256), F32), vm((2, 1, D), F32),
        vm((MP, 8, 128), F32), vm((128, 128), F32), vm((2, SEQ, 128), F32), vm((2, SEQ, 128), F32),
        vm((NZ, 2, PAYH, WIDE), I16), vm((NZ, 2, PAYH, WIDE), I16),
        vm((NZ, 2, PAY, WIDE), I16), vm((NZ, 2, PAY, WIDE), I16),
        vm((2, PAYH, WIDE), I16), vm((2, PAYH, WIDE), I16),
        vm((NZ, PAY, WIDE), I16), vm((NZ, PAY, WIDE), I16),
        vm((2, BLK // 2 + 16, THIN), I16), vm((2, BLK // 2 + 16, THIN), I16),
        vm((NZ, BLK + 16, THIN), I16), vm((NZ, BLK + 16, THIN), I16),
        vm((2, PAYH, THIN), I16), vm((2, PAYH, THIN), I16), vm((2, PAY, THIN), I16), vm((2, PAY, THIN), I16),
        sems((3,)), sems((2,)), sems((NZ,)),
        sems((NZ, 8)), sems((NZ, 8)), sems((NY - 1,)), sems((NY,)), sems((4, 2)), sems((4, 2)),
        sems((MP - 1,)), sems((MP,)), sems((NY - 1,)), sems((NY,)), sems((NZ - 1,)), sems((NZ,)),
        sems((MP - 1,)), sems((MP,)), sems((MP - 1,)), sems((MP,)), sems((MP - 1,)), sems((MP,)),
        sems((NZ, 2)), sems((NZ, 2)), sems((NZ, 2)), sems((NZ, 2)),
        sems((2,)), sems((2,)), sems((NZ,)), sems((NZ,)),
        sems((2,)), sems((2,)), sems((NZ,)), sems((NZ,)), sems((2,)), sems((2,)), sems((2,)), sems((2,)),
        sems((4, 2)), sems((4, 2)), sems((NZ, 2)), sems((NZ, 2)), sems((2,)), sems((2,)),
    ]
    context_grad, weight_grad, stream_grad = pl.pallas_call(
        kernel,
        out_shape=(
            jax.ShapeDtypeStruct(context.shape, BF16),
            jax.ShapeDtypeStruct((PART, HEADS), F32),
            jax.ShapeDtypeStruct(stream.shape, BF16),
        ),
        in_specs=[
            anywhere, anywhere, anywhere,
            pl.BlockSpec(memory_space=pltpu.VMEM),
            pl.BlockSpec(memory_space=pltpu.SMEM),
        ],
        out_specs=[anywhere] * 3,
        scratch_shapes=scratch,
        compiler_params=pltpu.CompilerParams(
            collective_id=0, has_side_effects=True, vmem_limit_bytes=60 * 2**20
        ),
        cost_estimate=pl.CostEstimate(flops=10**10, bytes_accessed=6 * 10**6, transcendentals=0),
    )(context, w_out.T, stream, gain.reshape(MP, BLK), partner)
    context_grad, weight_grad, stream_grad = pl.pallas_call(
        copy_out,
        out_shape=tuple(jax.ShapeDtypeStruct(a.shape, a.dtype) for a in (context_grad, weight_grad, stream_grad)),
        in_specs=[anywhere] * 3,
        out_specs=[anywhere] * 3,
        scratch_shapes=[vm(context.shape, BF16), vm((PART, HEADS), F32), vm(stream.shape, BF16), sems((5,)), sems((5,))],
    )(context_grad, weight_grad, stream_grad)
    return context_grad, weight_grad.T, stream_grad


def solution(mesh):
    placed = (P("dp", None, "mp"), P("mp", "dp"), P("dp", "mp", None), P(), P())
    return jax.shard_map(
        local,
        mesh=mesh,
        in_specs=placed,
        out_specs=(P("dp", None, "mp"), P("mp", "dp"), P("dp", "mp", None)),
        check_vma=False,
    )
```

```python
import jax
import jax.numpy as jnp
from jax import lax
from jax.experimental import pallas as pl
from jax.experimental.pallas import tpu as pltpu
from jax.sharding import PartitionSpec as P

EPS = 1e-06
SHARP = 10.0
LOSS_MUL = 512.0
D = 6144
SEQ = 512
HEADS = 384
VIEWS = 64
NZ, NY, NX = 8, 4, 4
MP = 8
OWN = 64
BLK = 768
PART = 192
HALF = PART // 2
PAY = PART + 16
PAYH = HALF + 16
WIDE = 256
THIN = HEADS - WIDE
F32 = jnp.float32
BF16 = jnp.bfloat16
I16 = jnp.int16
HIGH = lax.Precision.HIGHEST


def encode(values):
    top = jnp.max(jnp.abs(values), axis=0, keepdims=True)
    expo = jnp.ceil(16.0 * jnp.log2(jnp.maximum(top, 1e-30)))
    whole = jnp.round(values * jnp.exp2(14.9 - expo * 0.0625)).astype(jnp.int32).astype(I16)
    tail = jnp.broadcast_to(expo, (16, values.shape[1])).astype(jnp.int32).astype(I16)
    return whole, tail


def decode(ref, rows):
    expo = ref[pl.ds(rows, 16), :].astype(jnp.int32).astype(F32)[0:1, :]
    return ref[pl.ds(0, rows), :].astype(jnp.int32).astype(F32) * jnp.exp2(expo * 0.0625 - 14.9)


def put(ref, values, rows):
    whole, tail = encode(values)
    ref[pl.ds(0, rows), :] = whole
    ref[pl.ds(rows, 16), :] = tail


def kernel(
    ctx_hbm, w_hbm, stream_hbm, gain_ref, partner_ref,
    cg_hbm, wg_hbm, sg_hbm,
    G, SG, WT, CTX, CG, CGO, PB, WGO,
    EX1, UN, YB, ZB, E, LB, UPM, UPF, TM, TT, RB, CB,
    YS0, YR0, YS1, YR1, ZS0, ZR0, ZS1, ZR1,
    BZS0, BZR0, BZS1, BZR1, BYS0, BYR0, BYS1, BYR1,
    GA, in_sem, out_sem, sgo_sem,
    xs_s, x_r, wy_s, wy_r, wz_s, wz_r,
    e1_s, e1_r, ey_s, ey_r, ez_s, ez_r, el_s, el_r, eu_s, eu_r, et_s, et_r,
    ys0_s, ys0_r, ys1_s, ys1_r, zs0_s, zs0_r, zs1_s, zs1_r,
    bz0_s, bz0_r, bz1_s, bz1_r, by0_s, by0_r, by1_s, by1_r,
    vz_s, vz_r, vw_s, vw_r, vy_s, vy_r,
):
    dp = lax.axis_index("dp")
    mp = lax.axis_index("mp")
    z, y = lax.div(dp, NY), lax.rem(dp, NY)
    x, core = lax.div(mp, 2), lax.rem(mp, 2)

    def zy(dz, dy):
        return lax.rem(z + (dz + NZ), NZ) * NY + lax.rem(y + (dy + NY), NY)

    def slot(dx, other):
        c = 1 - core if other else core
        return lax.rem(x + (dx + NX), NX) * 2 + c

    def near(dx=0, other=False, dz=0, dy=0):
        return (zy(dz, dy), slot(dx, other))

    def remote(src, dst, ss, rs, dev):
        return pltpu.make_async_remote_copy(
            src_ref=src, dst_ref=dst, send_sem=ss, recv_sem=rs,
            device_id=dev, device_id_type=pl.DeviceIdType.MESH,
        )

    own_rows = pl.ds(pl.multiple_of(mp * OWN, OWN), OWN)
    load_stream = pltpu.make_async_copy(stream_hbm, G.at[:, own_rows, :], in_sem.at[0])
    load_ctx = pltpu.make_async_copy(ctx_hbm, CTX, in_sem.at[1])
    load_w = pltpu.make_async_copy(
        w_hbm, WT.at[z, y], in_sem.at[2]
    )
    load_stream.start()
    load_w.start()
    load_ctx.start()

    barrier = pltpu.get_barrier_semaphore()
    peers = [(dp, lax.rem(mp + d, MP)) for d in range(1, MP)]
    ypeers = [near(dy=d) for d in range(1, NY)]
    zpeers = [near(dz=d) for d in range(1, NZ)]
    for dev in peers + ypeers + zpeers:
        pl.semaphore_signal(barrier, inc=1, device_id=dev, device_id_type=pl.DeviceIdType.MESH)

    def zblock(k):
        dist = lax.div(NZ - k, 2)
        odd = lax.rem(k, 2)
        return lax.rem(z + NZ + (2 * odd - 1) * dist, NZ)

    def cols(k):
        return pl.ds(pl.multiple_of(zblock(k) * BLK, BLK), BLK)

    def rows(s):
        return pl.ds(pl.multiple_of(s * OWN, OWN), OWN)

    def x_own(k, t):
        ref = G.at[:, own_rows, cols(k)]
        dev = (near(dx=1), near(dx=-1), near(other=True))[t]
        return remote(ref, ref, xs_s.at[k, t], x_r.at[k, t], dev)

    def x_fwd(k, t):
        if t == 0:
            ref = G.at[0, rows(slot(-1, False)), cols(k)]
            return remote(ref, ref, xs_s.at[k, 3], x_r.at[k, 3], near(dx=1))
        ref = G.at[1, rows(slot(1, False)), cols(k)]
        return remote(ref, ref, xs_s.at[k, 4], x_r.at[k, 4], near(dx=-1))

    def x_sib(k, t):
        ref = G.at[:, rows(slot((-1, 1, 2)[t], False)), cols(k)]
        return remote(ref, ref, xs_s.at[k, 5 + t], x_r.at[k, 5 + t], near(other=True))

    def x_wait(k, t):
        if t < 3:
            ref = G.at[:, rows((slot(-1, False), slot(1, False), slot(0, True))[t]), cols(k)]
        elif t < 5:
            ref = G.at[t - 3, rows(slot(2, False)), cols(k)]
        else:
            ref = G.at[:, rows(slot((-1, 1, 2)[t - 5], True)), cols(k)]
        remote(ref, ref, xs_s.at[k, t], x_r.at[k, t], near(other=True)).wait_recv()

    def x_send(k):
        for t in range(3):
            x_own(k, t).start()

    def x_forward(k):
        x_wait(k, 0)
        x_fwd(k, 0).start()
        x_sib(k, 0).start()
        x_wait(k, 1)
        x_fwd(k, 1).start()
        x_sib(k, 1).start()

    def x_opposite(k):
        x_wait(k, 3)
        x_wait(k, 4)
        x_sib(k, 2).start()

    def x_arrived(k):
        x_wait(k, 2)
        for t in (5, 6, 7):
            x_wait(k, t)

    def wy_copy(d):
        ref = WT.at[z, y, pl.ds(0, HALF), :]
        return remote(ref, ref, wy_s.at[d - 1], wy_r.at[y], near(dy=d))

    def wy_wait(d):
        s = lax.rem(y + d, NY)
        ref = WT.at[z, s, pl.ds(0, HALF), :]
        remote(ref, ref, wy_s.at[d - 1], wy_r.at[s], near(dy=d)).wait_recv()

    def wz_ref(bundle, f, t):
        if f == 3:
            return WT.at[bundle, pl.ds(2 * t, 2), pl.ds(0, HALF), :]
        return WT.at[bundle, :, pl.ds(0, HALF), :]

    def wz_copy(f, t):
        step = f if t else NZ - f
        ref = wz_ref(lax.rem(z + step, NZ), f, t)
        return remote(ref, ref, wz_s.at[f, t], wz_r.at[f, t], near(dz=-1 if t else 1))

    def wz_wait(f, t):
        step = f + 1 if t else NZ - f - 1
        ref = wz_ref(lax.rem(z + step, NZ), f, t)
        remote(ref, ref, wz_s.at[f, t], wz_r.at[f, t], near(dz=1)).wait_recv()

    def vz_ref(bundle, f, t):
        if f == 3:
            return WT.at[bundle, y, pl.ds(HALF + t * (HALF // 2), HALF // 2), :]
        return WT.at[bundle, y, pl.ds(HALF, HALF), :]

    def vz_copy(f, t):
        step = f if t else NZ - f
        ref = vz_ref(lax.rem(z + step, NZ), f, t)
        return remote(ref, ref, vz_s.at[f, t], vz_r.at[f, t], near(dz=-1 if t else 1))

    def vz_wait(f, t):
        step = f + 1 if t else NZ - f - 1
        ref = vz_ref(lax.rem(z + step, NZ), f, t)
        remote(ref, ref, vz_s.at[f, t], vz_r.at[f, t], near(dz=1)).wait_recv()

    def vw_ref(n, dy):
        return WT.at[lax.rem(z + NZ - n, NZ), lax.rem(y + NY + dy, NY), pl.ds(HALF, HALF), :]

    def vw_copy(n, t):
        ref = vw_ref(n, 0)
        return remote(ref, ref, vw_s.at[n, t], vw_r.at[n, t], near(dy=-1 if t else 1))

    def vw_wait(n, t):
        ref = vw_ref(n, 1 if t else -1)
        remote(ref, ref, vw_s.at[n, t], vw_r.at[n, t], near(dy=1)).wait_recv()

    def vw_send(n):
        for t in range(2):
            vw_copy(n, t).start()

    def vz_next(f):
        for t in range(2):
            vz_wait(f - 1, t)
            vz_copy(f, t).start()
            vw_send(NZ - f if t else f)

    def vy_ref(dy, part):
        s = lax.rem(y + NY + dy, NY)
        return WT.at[pl.ds(part * (NZ // 2), NZ // 2), s, pl.ds(HALF, HALF), :]

    def vy_copy(t):
        ref = vy_ref(1 if t else -1, t)
        return remote(ref, ref, vy_s.at[t], vy_r.at[t], near(dy=-1 if t else 1))

    def vy_wait(t):
        ref = vy_ref(2, t)
        remote(ref, ref, vy_s.at[t], vy_r.at[t], near(dy=1)).wait_recv()

    def vy_begin():
        for t in range(2):
            vz_wait(3, t)
        vw_send(NZ // 2)

    def vy_next():
        for t in range(2):
            for n in range(NZ):
                vw_wait(n, t)
            vy_copy(t).start()

    def wz_next(f):
        for t in range(2):
            wz_wait(f - 1, t)
            wz_copy(f, t).start()

    def ex(buf, ss, rs, d):
        ref = buf.at[mp]
        return remote(ref, ref, ss.at[d - 1], rs.at[mp], (dp, lax.rem(mp + d, MP)))

    def ex_send(buf, ss, rs):
        for d in (4, 2, 3, 5, 6, 7, 1):
            ex(buf, ss, rs, d).start()

    def ex_wait(buf, ss, rs):
        for d in range(1, MP):
            s = lax.rem(mp + d, MP)
            ref = buf.at[s]
            remote(ref, ref, ss.at[d - 1], rs.at[s], (dp, s)).wait_recv()

    def ey_copy(d):
        ref = YB.at[y]
        return remote(ref, ref, ey_s.at[d - 1], ey_r.at[y], near(dy=d))

    def ez_copy(d):
        ref = ZB.at[z]
        return remote(ref, ref, ez_s.at[d - 1], ez_r.at[z], near(dz=d))

    load_stream.wait()

    def rstd_of(v):
        acc = jnp.zeros((OWN, 128), F32)
        for q in range(D // 128):
            part = G[v, own_rows, pl.ds(q * 128, 128)].astype(F32)
            acc = acc + part * part
        mean = jnp.sum(acc, axis=1, keepdims=True) * (1.0 / D)
        return lax.rsqrt(mean + EPS)

    rstd = [rstd_of(v) for v in range(2)]
    for v in range(2):
        for q in range(MP):
            part = G[v, own_rows, pl.ds(q * BLK, BLK)].astype(F32)
            EX1[mp, v, pl.ds(q, 1), :] = jnp.sum(part * rstd[v], axis=0, keepdims=True)

    pl.semaphore_wait(barrier, (MP - 1) + (NY - 1) + (NZ - 1))
    ex_send(EX1, e1_s, e1_r)
    load_w.wait()
    for d in (2, 1, 3):
        wy_copy(d).start()
    for t in range(2):
        vz_copy(0, t).start()
    vw_send(0)
    x_send(0)
    x_send(1)
    ex_wait(EX1, e1_s, e1_r)

    for q in range(MP):
        GA[pl.ds(q, 1), :] = gain_ref[pl.ds(q * BLK, BLK)].reshape(1, BLK)
    gain8 = GA[...]
    squares = []
    for v in range(2):
        total = EX1[0, v]
        for s in range(1, MP):
            total = total + EX1[s, v]
        pooled = total * gain8 * (1.0 / SEQ)
        UN[v] = pooled
        sq = jnp.sum(jnp.sum(pooled * pooled, axis=1, keepdims=True), axis=0, keepdims=True)
        squares.append(lax.rsqrt(sq + EPS))
    unit = [UN[v, pl.ds(mp, 1), :] * squares[v] for v in range(2)]
    emb = [u.astype(BF16).astype(F32) for u in unit]
    row8 = lax.broadcasted_iota(jnp.int32, (8, BLK), 0)
    zero8 = jnp.zeros((8, BLK), F32)

    def two(a, b, first):
        return jnp.where(row8 == first, a, jnp.where(row8 == first + 1, b, zero8))

    YB[y] = two(emb[0], emb[1], 2 * y)
    for d in (2, 1, 3):
        ey_copy(d).start()
    unit8 = two(unit[0], unit[1], 0)
    for d in range(1, NY):
        s = lax.rem(y + d, NY)
        ref = YB.at[s]
        remote(ref, ref, ey_s.at[d - 1], ey_r.at[s], near(dy=d)).wait_recv()
    eight = YB[0] + YB[1] + YB[2] + YB[3]
    ZB[z] = jnp.concatenate([eight[:, 0:HEADS], eight[:, HEADS:BLK]], axis=0).astype(BF16)
    for d in (4, 3, 5, 2, 6, 1, 7):
        ez_copy(d).start()
    vz_next(1)
    for d in range(1, NY):
        wy_wait(d)
    for t in range(2):
        wz_copy(0, t).start()
    x_forward(0)
    x_send(2)
    for d in range(1, NZ):
        s = lax.rem(z + d, NZ)
        ref = ZB.at[s]
        remote(ref, ref, ez_s.at[d - 1], ez_r.at[s], near(dz=d)).wait_recv()
    for s in range(NZ):
        part = ZB[s].astype(F32)
        E[pl.ds(8 * s, 8), pl.ds(0, HEADS)] = part[0:8]
        E[pl.ds(8 * s, 8), pl.ds(HEADS, HEADS)] = part[8:16]

    every = E[...]
    small = every.astype(BF16)
    contract = (((1,), (1,)), ((), ()))
    raw = lax.dot_general(small, small, contract, preferred_element_type=F32)
    cross = lax.dot_general(unit8, every, contract, precision=HIGH, preferred_element_type=F32)
    LB[mp, pl.ds(0, 32), pl.ds(0, 64)] = raw[0:32]
    LB[mp, pl.ds(0, 32), pl.ds(64, 64)] = raw[32:64]
    LB[mp, pl.ds(32, 8), pl.ds(0, 64)] = cross
    LB[mp, pl.ds(32, 8), pl.ds(64, 64)] = jnp.zeros((8, 64), F32)
    ex_send(LB, el_s, el_r)
    vz_next(2)
    wz_next(1)
    x_forward(1)
    x_opposite(0)
    x_send(3)
    ex_wait(LB, el_s, el_r)
    summed = LB[0]
    for s in range(1, MP):
        summed = summed + LB[s]
    logits = SHARP * jnp.concatenate([summed[0:32, 0:64], summed[0:32, 64:128]], axis=0)
    cross = summed[32:40, 0:64]

    rowi = lax.broadcasted_iota(jnp.int32, (VIEWS, VIEWS), 0)
    coli = lax.broadcasted_iota(jnp.int32, (VIEWS, VIEWS), 1)
    expo = jnp.where(rowi == coli, jnp.float32(0.0), jnp.exp(logits))
    both = expo / jnp.sum(expo, axis=1, keepdims=True) + expo / jnp.sum(expo, axis=0, keepdims=True)
    lane = lax.broadcasted_iota(jnp.int32, (1, VIEWS), 1)
    coef = []
    for v in range(2):
        index = 2 * dp + v
        mine = jnp.sum(jnp.where(rowi == index, both, 0.0), axis=0, keepdims=True)
        target = jnp.where(lane == partner_ref[index], jnp.float32(2.0), jnp.float32(0.0))
        coef.append(LOSS_MUL * (mine - target))
    r64 = lax.broadcasted_iota(jnp.int32, (8, VIEWS), 0)
    coef8 = jnp.where(r64 == 0, coef[0], jnp.where(r64 == 1, coef[1], jnp.zeros((8, VIEWS), F32)))
    demb = SHARP * jnp.dot(coef8, every, precision=HIGH, preferred_element_type=F32)
    along = SHARP * jnp.sum(coef8 * cross, axis=1, keepdims=True)
    inv8 = two(jnp.broadcast_to(squares[0], (1, BLK)), jnp.broadcast_to(squares[1], (1, BLK)), 0)
    dpooled = inv8 * (demb - unit8 * along)
    up8 = GA[pl.ds(mp, 1), :] * dpooled * (1.0 / SEQ)
    UPM[mp] = jnp.zeros((8, 256), F32)
    for v in range(2):
        for c in range(3):
            UPM[mp, pl.ds(3 * v + c, 1), :] = up8[v : v + 1, 256 * c : 256 * (c + 1)]
    ex_send(UPM, eu_s, eu_r)
    x_forward(2)
    x_opposite(1)
    x_send(4)
    vz_next(3)
    ex_wait(UPM, eu_s, eu_r)
    for s in range(MP):
        for v in range(2):
            for c in range(3):
                UPF[v, :, pl.ds(s * BLK + 256 * c, 256)] = UPM[s, pl.ds(3 * v + c, 1), :]

    diag = lax.broadcasted_iota(jnp.int32, (OWN, OWN), 0) == lax.broadcasted_iota(jnp.int32, (OWN, OWN), 1)
    TM[mp] = jnp.zeros((8, 128), F32)
    for v in range(2):
        acc = jnp.zeros((OWN, 128), F32)
        for q in range(D // 128):
            part = G[v, own_rows, pl.ds(q * 128, 128)].astype(F32)
            acc = acc + part * UPF[v, :, pl.ds(q * 128, 128)]
        inner = jnp.sum(acc, axis=1, keepdims=True) * (1.0 / D)
        slope = rstd[v] * rstd[v] * rstd[v] * inner
        for r, column in enumerate((rstd[v], slope)):
            line = jnp.sum(jnp.where(diag, column, 0.0), axis=0, keepdims=True)
            TM[mp, pl.ds(r, 1), pl.ds(v * OWN, OWN)] = line
    ex_send(TM, et_s, et_r)
    vy_begin()
    wz_next(2)
    x_forward(3)
    x_opposite(2)
    x_send(5)
    load_ctx.wait()
    CG[...] = jnp.zeros_like(CG)
    ex_wait(TM, et_s, et_r)
    for s in range(MP):
        TT[pl.ds(8 * s, 8), :] = TM[s]
    TT[pl.ds(64, 64), :] = jnp.zeros((64, 128), F32)
    flat = TT[...].T
    for s in range(MP):
        for v in range(2):
            piece = flat[v * OWN : (v + 1) * OWN]
            RB[v, pl.ds(s * OWN, OWN), :] = jnp.broadcast_to(piece[:, 8 * s : 8 * s + 1], (OWN, 128))
            CB[v, pl.ds(s * OWN, OWN), :] = jnp.broadcast_to(piece[:, 8 * s + 1 : 8 * s + 2], (OWN, 128))

    wide, thin = pl.ds(0, WIDE), pl.ds(WIDE, THIN)

    def part_rows(dy):
        return pl.ds(pl.multiple_of(lax.rem(y + dy, NY) * PART, PART), PART)

    def half_rows(dy, h):
        start = lax.rem(y + dy, NY) * PART + h * HALF
        return pl.ds(pl.multiple_of(start, HALF), HALF)

    def ys0(k, h):
        return remote(YS0.at[k, h], YR0.at[k, h], ys0_s.at[k, h], ys0_r.at[k, h], near(dy=1 if h == 0 else -1))

    def ys1(k, h):
        return remote(YS1.at[k, h], YR1.at[k, h], ys1_s.at[k, h], ys1_r.at[k, h], near(dy=1 if h == 0 else -1))

    def zs0(h):
        return remote(ZS0.at[h], ZR0.at[h], zs0_s.at[h], zs0_r.at[h], near(dz=1 if h == 0 else -1))

    def zs1(k):
        odd = lax.rem(k, 2)
        target = lax.rem(z + NZ - 1 + 2 * odd, NZ) * NY + y
        return remote(ZS1.at[k], ZR1.at[k], zs1_s.at[k], zs1_r.at[k], (target, mp))

    def sgout(k):
        return pltpu.make_async_copy(SG.at[:, own_rows, cols(k)], sg_hbm.at[:, :, cols(k)], sgo_sem.at[k])

    def block(k):
        first = zblock(k) * BLK
        x_arrived(k)

        def build(g, carry):
            v = lax.div(g, MP)
            r = rows(lax.rem(g, MP))
            rs = RB[v, r, :]
            cs = CB[v, r, :]
            for l in range(BLK // 128):
                c = pl.ds(pl.multiple_of(first + l * 128, 128), 128)
                value = G[v, r, c].astype(F32)
                SG[v, r, c] = (rs * UPF[v, :, c] - value * cs).astype(BF16)
            return carry

        lax.fori_loop(0, 2 * MP, build, 0)
        sgout(k).start()
        keep = lax.rem(k, 5)

        left = SG[:, :, pl.ds(pl.multiple_of(first, BLK), BLK)].reshape(2 * SEQ, BLK)
        right = CTX[...].reshape(2 * SEQ, HEADS)
        PB[keep] = lax.dot_general(left, right, (((0,), (0,)), ((), ())), preferred_element_type=F32)
        for h in range(2):
            put(YS0.at[k, h], PB[keep, half_rows(2, h), wide], HALF)
            ys0(k, h).start()

    def y_second(k):
        keep = lax.rem(k, 5)
        for h in range(2):
            ys0(k, h).wait_recv()
            spot = half_rows(1 if h == 0 else 3, h)
            PB[keep, spot, wide] = PB[keep, spot, wide] + decode(YR0.at[k, h], HALF)
            put(YS1.at[k, h], PB[keep, part_rows(1 if h == 0 else 3), wide], PART)
            ys1(k, h).start()

    def z_part(k):
        keep = lax.rem(k, 5)
        ys1(k, 0).wait_recv()
        ys1(k, 1).wait_recv()
        spot = part_rows(0)
        PB[keep, spot, wide] = PB[keep, spot, wide] + decode(YR1.at[k, 0], PART) + decode(YR1.at[k, 1], PART)

        @pl.when(k == 0)
        def _():
            for h in range(2):
                put(ZS0.at[h], PB[keep, half_rows(0, h), wide], HALF)
                zs0(h).start()

        for h in range(2):
            @pl.when(k == 1 + h)
            def _():
                zs0(h).wait_recv()
                half = half_rows(0, h)
                PB[keep, half, wide] = PB[keep, half, wide] + decode(ZR0.at[h], HALF)

        @pl.when(jnp.logical_and(k >= 3, k <= 6))
        def _():
            zs1(k - 2).wait_recv()
            PB[keep, spot, wide] = PB[keep, spot, wide] + decode(ZR1.at[k - 2], PART)

        @pl.when(jnp.logical_and(k >= 1, k <= 6))
        def _():
            put(ZS1.at[k], PB[keep, spot, wide], PART)
            zs1(k).start()

        @pl.when(k == 7)
        def _():
            zs1(5).wait_recv()
            zs1(6).wait_recv()
            WGO[:, wide] = PB[keep, spot, wide] + decode(ZR1.at[5], PART) + decode(ZR1.at[6], PART)

    def bz0(h):
        return remote(BZS0.at[h], BZR0.at[h], bz0_s.at[h], bz0_r.at[h], near(dz=1 if h == 0 else -1))

    def bz1(k):
        odd = lax.rem(k, 2)
        target = lax.rem(z + NZ - 1 + 2 * odd, NZ) * NY + y
        return remote(BZS1.at[k], BZR1.at[k], bz1_s.at[k], bz1_r.at[k], (target, mp))

    def by0(h):
        return remote(BYS0.at[h], BYR0.at[h], by0_s.at[h], by0_r.at[h], near(dy=1 if h == 0 else -1))

    def by1(h):
        return remote(BYS1.at[h], BYR1.at[h], by1_s.at[h], by1_r.at[h], near(dy=1 if h == 0 else -1))

    def b_part(k):
        keep = lax.rem(k, 5)

        @pl.when(k == 0)
        def _():
            for h in range(2):
                put(BZS0.at[h], PB[keep, pl.ds(h * BLK // 2, BLK // 2), thin], BLK // 2)
                bz0(h).start()

        for h in range(2):
            @pl.when(k == 1 + h)
            def _():
                bz0(h).wait_recv()
                half = pl.ds(h * BLK // 2, BLK // 2)
                PB[keep, half, thin] = PB[keep, half, thin] + decode(BZR0.at[h], BLK // 2)

        @pl.when(jnp.logical_and(k >= 3, k <= 6))
        def _():
            bz1(k - 2).wait_recv()
            PB[keep, :, thin] = PB[keep, :, thin] + decode(BZR1.at[k - 2], BLK)

        @pl.when(jnp.logical_and(k >= 1, k <= 6))
        def _():
            put(BZS1.at[k], PB[keep, :, thin], BLK)
            bz1(k).start()

        @pl.when(k == 7)
        def _():
            bz1(5).wait_recv()
            bz1(6).wait_recv()
            PB[keep, :, thin] = PB[keep, :, thin] + decode(BZR1.at[5], BLK) + decode(BZR1.at[6], BLK)
            for h in range(2):
                put(BYS0.at[h], PB[keep, half_rows(2, h), thin], HALF)
                by0(h).start()

    def b_second():
        for h in range(2):
            by0(h).wait_recv()
            spot = half_rows(1 if h == 0 else 3, h)
            PB[2, spot, thin] = PB[2, spot, thin] + decode(BYR0.at[h], HALF)
            put(BYS1.at[h], PB[2, part_rows(1 if h == 0 else 3), thin], PART)
            by1(h).start()

    def b_last():
        by1(0).wait_recv()
        by1(1).wait_recv()
        WGO[:, thin] = PB[2, part_rows(0), thin] + decode(BYR1.at[0], PART) + decode(BYR1.at[1], PART)

    def project(b):
        first = zblock(b) * BLK

        left = SG[:, :, pl.ds(pl.multiple_of(first, BLK), BLK)].reshape(2 * SEQ, BLK)
        right = WT[zblock(b)].reshape(BLK, HEADS)
        update = jnp.dot(left, right, preferred_element_type=F32)
        CG[...] = CG[...] + update.reshape(2, SEQ, HEADS)

    def iteration(k, carry):
        @pl.when(k <= 1)
        def _():
            x_send(k + 6)

        @pl.when(k <= 3)
        def _():
            x_forward(k + 4)

        @pl.when(k <= 4)
        def _():
            x_opposite(k + 3)

        @pl.when(k == 1)
        def _():
            wz_next(3)

        @pl.when(k == 0)
        def _():
            vy_next()

        @pl.when(k == 4)
        def _():
            for t in range(2):
                wz_wait(3, t)
                vy_wait(t)

        @pl.when(k <= 7)
        def _():
            block(k)

        @pl.when(jnp.logical_and(k >= 1, k <= 8))
        def _():
            b_part(k - 1)

        @pl.when(jnp.logical_and(k >= 2, k <= 9))
        def _():
            y_second(k - 2)

        @pl.when(k >= 4)
        def _():
            z_part(k - 4)

        @pl.when(jnp.logical_and(k >= 4, k <= 5))
        def _():
            project(k - 1)

        @pl.when(jnp.logical_and(k >= 6, k <= 7))
        def _():
            project(k - 5)

        @pl.when(k == 8)
        def _():
            project(5)
            project(6)

        @pl.when(k == 9)
        def _():
            b_second()
            project(7)
            project(0)
            CGO[...] = CG[...].astype(BF16)
            pltpu.make_async_copy(CGO, cg_hbm, out_sem.at[0]).start()

        return carry

    lax.fori_loop(0, 12, iteration, 0)
    b_last()
    wg_out = pltpu.make_async_copy(WGO, wg_hbm, out_sem.at[1])
    wg_out.start()

    def drain(k, carry):
        for t in range(3):
            x_own(k, t).wait_send()
            x_sib(k, t).wait_send()
        for h in range(2):
            x_fwd(k, h).wait_send()
            ys0(k, h).wait_send()
            ys1(k, h).wait_send()
        sgout(k).wait()

        @pl.when(jnp.logical_and(k >= 1, k <= 6))
        def _():
            zs1(k).wait_send()
            bz1(k).wait_send()

        return carry

    lax.fori_loop(0, NZ, drain, 0)
    for h in range(2):
        zs0(h).wait_send()
        bz0(h).wait_send()
        by0(h).wait_send()
        by1(h).wait_send()
        vy_copy(h).wait_send()
        for n in range(NZ):
            vw_copy(n, h).wait_send()
    for d in range(1, NY):
        wy_copy(d).wait_send()
        ey_copy(d).wait_send()
    for f in range(4):
        for t in range(2):
            wz_copy(f, t).wait_send()
            vz_copy(f, t).wait_send()
    for d in range(1, NZ):
        ez_copy(d).wait_send()
    for d in range(1, MP):
        ex(EX1, e1_s, e1_r, d).wait_send()
        ex(LB, el_s, el_r, d).wait_send()
        ex(UPM, eu_s, eu_r, d).wait_send()
        ex(TM, et_s, et_r, d).wait_send()
    pltpu.make_async_copy(CGO, cg_hbm, out_sem.at[0]).wait()
    wg_out.wait()


def copy_out(cg, wg, sg, cg_out, wg_out, sg_out, cg_mid, wg_mid, sg_mid, sem_in, sem_out):
    moves = [(sg, sg_mid, sg_out, v) for v in range(2)] + [(cg, cg_mid, cg_out, v) for v in range(2)]
    moves = [(a.at[v], b.at[v], c.at[v]) for a, b, c, v in moves] + [(wg, wg_mid, wg_out)]
    loads = [pltpu.make_async_copy(a, b, sem_in.at[n]) for n, (a, b, c) in enumerate(moves)]
    stores = [pltpu.make_async_copy(b, c, sem_out.at[n]) for n, (a, b, c) in enumerate(moves)]
    for load in loads:
        load.start()
    for load, store in zip(loads, stores):
        load.wait()
        store.start()
    for store in stores:
        store.wait()


def local(context, w_out, stream, gain, partner):
    anywhere = pl.BlockSpec(memory_space=pl.ANY)
    sems = pltpu.SemaphoreType.DMA
    vm = pltpu.VMEM
    scratch = [
        vm((2, SEQ, D), BF16), vm((2, SEQ, D), BF16), vm((NZ, NY, PART, HEADS), BF16), vm((2, SEQ, HEADS), BF16),
        vm((2, SEQ, HEADS), F32), vm((2, SEQ, HEADS), BF16), vm((5, BLK, HEADS), F32), vm((PART, HEADS), F32),
        vm((MP, 2, MP, BLK), F32), vm((2, MP, BLK), F32), vm((NY, 8, BLK), F32), vm((NZ, 16, HEADS), BF16),
        vm((VIEWS, BLK), F32), vm((MP, 40, 128), F32), vm((MP, 8, 256), F32), vm((2, 1, D), F32),
        vm((MP, 8, 128), F32), vm((128, 128), F32), vm((2, SEQ, 128), F32), vm((2, SEQ, 128), F32),
        vm((NZ, 2, PAYH, WIDE), I16), vm((NZ, 2, PAYH, WIDE), I16),
        vm((NZ, 2, PAY, WIDE), I16), vm((NZ, 2, PAY, WIDE), I16),
        vm((2, PAYH, WIDE), I16), vm((2, PAYH, WIDE), I16),
        vm((NZ, PAY, WIDE), I16), vm((NZ, PAY, WIDE), I16),
        vm((2, BLK // 2 + 16, THIN), I16), vm((2, BLK // 2 + 16, THIN), I16),
        vm((NZ, BLK + 16, THIN), I16), vm((NZ, BLK + 16, THIN), I16),
        vm((2, PAYH, THIN), I16), vm((2, PAYH, THIN), I16), vm((2, PAY, THIN), I16), vm((2, PAY, THIN), I16),
        vm((MP, BLK), F32), sems((3,)), sems((2,)), sems((NZ,)),
        sems((NZ, 8)), sems((NZ, 8)), sems((NY - 1,)), sems((NY,)), sems((4, 2)), sems((4, 2)),
        sems((MP - 1,)), sems((MP,)), sems((NY - 1,)), sems((NY,)), sems((NZ - 1,)), sems((NZ,)),
        sems((MP - 1,)), sems((MP,)), sems((MP - 1,)), sems((MP,)), sems((MP - 1,)), sems((MP,)),
        sems((NZ, 2)), sems((NZ, 2)), sems((NZ, 2)), sems((NZ, 2)),
        sems((2,)), sems((2,)), sems((NZ,)), sems((NZ,)),
        sems((2,)), sems((2,)), sems((NZ,)), sems((NZ,)), sems((2,)), sems((2,)), sems((2,)), sems((2,)),
        sems((4, 2)), sems((4, 2)), sems((NZ, 2)), sems((NZ, 2)), sems((2,)), sems((2,)),
    ]
    context_grad, weight_grad, stream_grad = pl.pallas_call(
        kernel,
        out_shape=(
            jax.ShapeDtypeStruct(context.shape, BF16),
            jax.ShapeDtypeStruct((PART, HEADS), F32),
            jax.ShapeDtypeStruct(stream.shape, BF16),
        ),
        in_specs=[
            anywhere, anywhere, anywhere,
            pl.BlockSpec(memory_space=pltpu.VMEM),
            pl.BlockSpec(memory_space=pltpu.SMEM),
        ],
        out_specs=[anywhere] * 3,
        scratch_shapes=scratch,
        compiler_params=pltpu.CompilerParams(
            collective_id=0, has_side_effects=True, vmem_limit_bytes=60 * 2**20
        ),
        cost_estimate=pl.CostEstimate(flops=10**10, bytes_accessed=6 * 10**6, transcendentals=0),
    )(context, w_out.T, stream, gain, partner)
    context_grad, weight_grad, stream_grad = pl.pallas_call(
        copy_out,
        out_shape=tuple(jax.ShapeDtypeStruct(a.shape, a.dtype) for a in (context_grad, weight_grad, stream_grad)),
        in_specs=[anywhere] * 3,
        out_specs=[anywhere] * 3,
        scratch_shapes=[vm(context.shape, BF16), vm((PART, HEADS), F32), vm(stream.shape, BF16), sems((5,)), sems((5,))],
    )(context_grad, weight_grad, stream_grad)
    return context_grad, weight_grad.T, stream_grad


def solution(mesh):
    placed = (P("dp", None, "mp"), P("mp", "dp"), P("dp", "mp", None), P(), P())
    return jax.shard_map(
        local,
        mesh=mesh,
        in_specs=placed,
        out_specs=(P("dp", None, "mp"), P("mp", "dp"), P("dp", "mp", None)),
        check_vma=False,
    )
```
